128 devices in a mesh: node: 16 (over x, z), local: 8 (over y, core).
Axes of the slice: x: 4, y: 4, z: 4, core: 2. Of those that a mesh axis runs over, the one named last changes fastest.
Arguments:
- tokens: bfloat16 [2048, 3584], P(('node', 'local')), may hold values from -6 to 6
- cotangent: bfloat16 [2048, 3584], P(('node', 'local')), may hold values from -0.59765625 to 0.59765625
- node_routes: int32 [2048, 4], P(('node', 'local')), may hold values from 0 to 15, all different within a row; in each aligned block of 16 rows (0 to 15, 16 to 31, ...) at most 5 rows name the same one
- home_local: int32 [128, 16], P(('node', 'local')), may hold values from 0 to 3
- second_local: int32 [2048, 4], P(('node', 'local')), may hold values from 0 to 3
- gate_weights: bfloat16 [2048, 8], P(('node', 'local')), may hold values from 0.049804688 to 0.5
- gate_w: bfloat16 [128, 3584, 512], P(('node', 'local')), may hold values from -0.09375 to 0.09375
- up_w: bfloat16 [128, 3584, 512], P(('node', 'local')), may hold values from -0.09375 to 0.09375
- down_w: bfloat16 [128, 512, 3584], P(('node', 'local')), may hold values from -0.1875 to 0.1875
Outputs:
- d_tokens: bfloat16 [2048, 3584], P(('node', 'local'))
- d_gates: bfloat16 [2048, 8], P(('node', 'local'))
- d_gate_w: bfloat16 [128, 3584, 512], P(('node', 'local'))
- d_up_w: bfloat16 [128, 3584, 512], P(('node', 'local'))
- d_down_w: bfloat16 [128, 512, 3584], P(('node', 'local'))
The draws below stay inside these ranges and needn't reach their ends.
Inputs may be any that keep to these rules, and one draw needn't show every extreme that they name: `node_routes`: each row names 4 different nodes; within the 16 rows of one device no node is named by more than 5 rows, a bound that some block reaches, so one device sends at most 5 rows to one node or one expert, and some device exactly 5.
All inputs are finite; a program needn't handle non-finite values.
Results may differ from the reference program's by a relative error of at most 0.014.
Values may be sent and summed in bfloat16 or wider, within the bound.
No kernel may reach another device: no remote copies, remote signals or barrier semaphores. Data moves between devices by JAX's collectives and lax.ppermute only.
A program may use at most 128 MiB of HBM per device.

```python
import math
import jax
import jax.numpy as jnp
import numpy as np
from jax import lax

D = 3584
H = 1024
HD = 512
TOP = 8
NODES_TOK = 4
TOK_DEV = 16
EXPERTS = 64
EPN = 4
SHARDS = 128
TOKENS = 2048
CAP = 5
N_NODE = 16
N_LOCAL = 8


def place_ends(result, own_key, smallest, top_value):
    place = [jax.random.randint(jax.random.fold_in(own_key, axis), (), 0, length) for axis, length in enumerate(result.shape)]
    longest = result.shape.index(max(result.shape))
    next_to = place[:longest] + [(place[longest] + 1) % result.shape[longest]] + place[longest + 1:]
    return result.at[tuple(place)].set(smallest).at[tuple(next_to)].set(top_value)


def levels(own_key, dims, shards, low, high):
    factor_of = 1.0
    for axis_at, blocks in shards:
        heights = jax.random.uniform(jax.random.fold_in(jax.random.fold_in(own_key, 6), axis_at), (blocks,), jnp.float32, low / len(shards), high / len(shards))
        factor_of = factor_of * jnp.repeat(jnp.exp(heights), dims[axis_at] // blocks).reshape((-1,) + (1,) * (len(dims) - 1 - axis_at))
    return factor_of


def deal_out(key, own, number, rows, number_of, top, limit, lean):
    order = jax.random.permutation(key, number_of)
    packed, usual = portions_of(number_of, rows * top, limit, lean, True), portions_of(number_of, rows * top, limit, lean, False)
    places = jnp.arange(number_of)

    def named(lengths, offset_by):
        used = int((lengths > 0).sum())
        fixed = max(1, used // 4)
        moved = fixed + (places - fixed + offset_by * (used - fixed)) % max(1, number_of - fixed)
        return jnp.zeros((number_of,), jnp.int32).at[order[jnp.where(places < fixed, places, moved)]].set(jnp.asarray(lengths, jnp.int32))

    lengths = jnp.where(number % 4 == 0, named(packed, number // 4), named(usual, number - number // 4 - 1))
    mixed = jax.random.permutation(jax.random.fold_in(own, 3), number_of)
    giver, sink = mixed[0:number_of // 2 * 2:2], mixed[1:number_of // 2 * 2:2]
    margin = jnp.minimum(lengths[giver] - 1, limit - lengths[sink]) // 2
    margin = jnp.where((giver == order[0]) | (sink == order[0]) | (lengths[sink] == 0), 0, jnp.maximum(margin, 0))
    moved = jax.random.randint(jax.random.fold_in(own, 4), (number_of // 2,), 0, 1 << 20) % (margin + 1)
    lengths = lengths.at[giver].add(-moved).at[sink].add(moved)
    members = jnp.searchsorted(jnp.cumsum(lengths), jnp.arange(rows * top), side="right").astype(jnp.int32)
    table = members.reshape(top, rows).T
    table = table[jax.random.permutation(jax.random.fold_in(own, 1), rows)]
    offset_by = jax.random.randint(jax.random.fold_in(own, 2), (rows, 1), 0, top)
    return jnp.take_along_axis(table, (jnp.arange(top)[None, :] + offset_by) % top, axis=1)


def portions_of(amount, total, bound, lean, full):
    portions = [(1 << 20) // math.isqrt(rank ** lean) + 1 for rank in range(1, amount + 1)]
    largest = bound if full else min(bound, max(-(-total // amount), total * portions[0] // sum(portions)))
    least = 1 if total - largest >= amount - 1 else 0
    holding, rest = [largest] + [least] * (amount - 1), total - largest - least * (amount - 1)
    while rest > 0:
        movable = [i for i in range(1, amount) if holding[i] < largest] or [i for i in range(1, amount) if holding[i] < bound]
        pool, left = sum([portions[i] for i in movable]), rest
        for i in movable:
            more = min(bound - holding[i], max(1, left * portions[i] // pool), rest)
            holding[i] = holding[i] + more
            rest = rest - more
    return np.array(holding)


def normal_values(own_key, shape, spread, limit, cuts=(), kind=jnp.bfloat16):
    loudness = levels(own_key, shape, cuts, -0.22, 0.18) if cuts else 1.0
    entries = jax.random.normal(own_key, shape, jnp.float32) * spread * loudness
    return jnp.minimum(jnp.maximum(entries, -limit), limit).astype(kind)


def setup_inputs(seed: int = 0) -> dict:
    key_list = jax.random.split(jax.random.key(seed), 10)
    tokens = normal_values(key_list[0], (TOKENS, D), 1.0, 6.0, ((0, 128),))
    cotangent = normal_values(key_list[1], (TOKENS, D), 0.1, 0.59765625, ((0, 128),))
    node_routes_keys = jax.random.split(jax.random.fold_in(key_list[2], 1), TOKENS // TOK_DEV)
    node_routes_turns = jax.random.permutation(jax.random.fold_in(key_list[2], 3), TOKENS // TOK_DEV)
    node_routes = jax.vmap(lambda own, number: deal_out(jax.random.fold_in(key_list[2], 2), own, number, TOK_DEV, N_NODE, NODES_TOK, CAP, 2))(node_routes_keys, node_routes_turns).reshape((TOKENS, NODES_TOK))
    home_local = place_ends(jax.random.randint(key_list[3], (SHARDS, N_NODE), 0, EPN), jax.random.fold_in(key_list[3], 1), 0, EPN - 1).astype(jnp.int32)
    second_local = place_ends(jax.random.randint(key_list[4], (TOKENS, NODES_TOK), 0, EPN), jax.random.fold_in(key_list[4], 1), 0, EPN - 1).astype(jnp.int32)
    gate_weights = jnp.clip(jnp.exp(math.log(0.5) - 2.306499 * jax.random.uniform(key_list[5], (TOKENS, TOP), jnp.float32) ** levels(key_list[5], (TOKENS, TOP), ((0, 128),), -0.2, 0.2)), 0.049804688, 0.5).astype(jnp.bfloat16)
    gate_w = normal_values(key_list[6], (SHARDS, D, HD), D ** -0.5, 0.09375, ((0, 128),))
    up_w = normal_values(key_list[7], (SHARDS, D, HD), D ** -0.5, 0.09375, ((0, 128),))
    down_w = normal_values(key_list[8], (SHARDS, HD, D), H ** -0.5, 0.1875, ((0, 128),))
    return dict(tokens=tokens, cotangent=cotangent, node_routes=node_routes, home_local=home_local, second_local=second_local, gate_weights=gate_weights, gate_w=gate_w, up_w=up_w, down_w=down_w)


def silu_parts(pre_gate):
    sigmoid = jax.nn.sigmoid(pre_gate)
    return pre_gate * sigmoid, sigmoid * (1.0 + pre_gate * (1.0 - sigmoid))


def route_experts(node_routes, home_local, second_local):
    per_node = N_LOCAL // 2
    source = jnp.arange(TOKENS, dtype=jnp.int32) // TOK_DEV
    home = home_local[source[:, None], node_routes]
    other = jnp.where(second_local == 0, (home + 1) % per_node, (home + second_local) % per_node)
    local_pick = jnp.stack([home, other], axis=2).reshape(TOKENS, TOP)
    nodes = jnp.repeat(node_routes, 2, axis=1)
    return (nodes * per_node + local_pick).astype(jnp.int32)


def reference(tokens, cotangent, node_routes, home_local, second_local, gate_weights, gate_w, up_w, down_w):
    expert_ids = route_experts(node_routes, home_local, second_local)
    onehot = (expert_ids[:, :, None] == jnp.arange(EXPERTS, dtype=jnp.int32)[None, None, :]).astype(jnp.int32)
    member = jnp.sum(onehot, axis=1).reshape(SHARDS, TOK_DEV, EXPERTS)
    rank_table = (jnp.cumsum(member, axis=1) - member).reshape(TOKENS, EXPERTS)
    slot_index = jnp.sum(onehot * rank_table[:, None, :], axis=2)
    source = (jnp.arange(TOKENS, dtype=jnp.int32) // TOK_DEV)[:, None]
    row_index = (source * CAP + slot_index).astype(jnp.int32)
    token_index = jnp.broadcast_to(jnp.arange(TOKENS, dtype=jnp.int32)[:, None], (TOKENS, TOP))
    slots = SHARDS * CAP
    token_table = jnp.full((EXPERTS, slots), TOKENS, jnp.int32).at[expert_ids, row_index].set(token_index)
    weight_table = jnp.zeros((EXPERTS, slots), jnp.float32).at[expert_ids, row_index].set(gate_weights.astype(jnp.float32))
    tokens_pad = jnp.concatenate([tokens, jnp.zeros((1, D), tokens.dtype)], axis=0)
    cotangent_pad = jnp.concatenate([cotangent, jnp.zeros((1, D), cotangent.dtype)], axis=0)
    gate_full = gate_w.reshape(EXPERTS, 2, D, HD)
    up_full = up_w.reshape(EXPERTS, 2, D, HD)
    down_full = down_w.reshape(EXPERTS, H, D)

    def one_expert(expert):
        rows_in = tokens_pad[token_table[expert]]
        grads_in = cotangent_pad[token_table[expert]]
        weights_in = weight_table[expert][:, None]
        gate_proj = jnp.transpose(gate_full[expert], (1, 0, 2)).reshape(D, H)
        up_proj = jnp.transpose(up_full[expert], (1, 0, 2)).reshape(D, H)
        down_proj = down_full[expert]
        pre_gate = jnp.dot(rows_in, gate_proj, preferred_element_type=jnp.float32)
        pre_up = jnp.dot(rows_in, up_proj, preferred_element_type=jnp.float32)
        activated, slope = silu_parts(pre_gate)
        hidden = (activated * pre_up).astype(jnp.bfloat16)
        hidden_grad = jnp.dot(grads_in, down_proj.T, preferred_element_type=jnp.float32)
        router_grad = jnp.sum(hidden_grad * hidden.astype(jnp.float32), axis=1).astype(jnp.bfloat16)
        weighted = weights_in * hidden_grad
        gate_grad = (weighted * pre_up * slope).astype(jnp.bfloat16)
        up_grad = (weighted * activated).astype(jnp.bfloat16)
        hidden_scaled = (weights_in * hidden.astype(jnp.float32)).astype(jnp.bfloat16)
        down_update = jnp.dot(hidden_scaled.T, grads_in, preferred_element_type=jnp.float32).astype(jnp.bfloat16)
        gate_update = jnp.dot(rows_in.T, gate_grad, preferred_element_type=jnp.float32).astype(jnp.bfloat16)
        up_update = jnp.dot(rows_in.T, up_grad, preferred_element_type=jnp.float32).astype(jnp.bfloat16)
        input_grad = jnp.dot(gate_grad, gate_proj.T, preferred_element_type=jnp.float32)
        input_grad = input_grad + jnp.dot(up_grad, up_proj.T, preferred_element_type=jnp.float32)
        return input_grad.astype(jnp.bfloat16), router_grad, gate_update, up_update, down_update

    input_rows, router_rows, gate_updates, up_updates, down_updates = lax.map(one_expert, jnp.arange(EXPERTS, dtype=jnp.int32))
    summed = jnp.zeros((TOKENS + 1, D), jnp.float32).at[token_table].add(input_rows.astype(jnp.float32))
    d_tokens = summed[:TOKENS].astype(jnp.bfloat16)
    d_gates = router_rows[expert_ids, row_index]
    d_gate_w = jnp.transpose(gate_updates.reshape(EXPERTS, D, 2, HD), (0, 2, 1, 3)).reshape(SHARDS, D, HD)
    d_up_w = jnp.transpose(up_updates.reshape(EXPERTS, D, 2, HD), (0, 2, 1, 3)).reshape(SHARDS, D, HD)
    d_down_w = down_updates.reshape(SHARDS, HD, D)
    return (d_tokens, d_gates, d_gate_w, d_up_w, d_down_w)
```

```python
import jax
import jax.numpy as jnp
from jax import lax
from jax.sharding import PartitionSpec as P

BF = jnp.bfloat16
F32 = jnp.float32
TAIL = 128


def along_x(value, step):
    pairs = [(x * 4 + z, (x + step) % 4 * 4 + z) for x in range(4) for z in range(4)]
    return lax.ppermute(value, "node", pairs)


def along_z(value, step):
    pairs = [(x * 4 + z, x * 4 + (z + step) % 4) for x in range(4) for z in range(4)]
    return lax.ppermute(value, "node", pairs)


def along_y(value, step):
    pairs = [(y * 2 + c, (y + step) % 4 * 2 + c) for y in range(4) for c in range(2)]
    return lax.ppermute(value, "local", pairs)


def across(value):
    return lax.ppermute(value, "local", [(i, i ^ 1) for i in range(8)])


def dot(left, right, dims):
    return lax.dot_general(left, right, ((dims[0], dims[1]), ((), ())), preferred_element_type=F32)


def silu_parts(pre_gate):
    sigmoid = jax.nn.sigmoid(pre_gate)
    return (pre_gate * sigmoid, sigmoid * (1.0 + pre_gate * (1.0 - sigmoid)))


def multicast_x(value):
    return jnp.concatenate(
        [value, along_x(value, 1), along_x(value, -1), along_x(value, 2)], axis=0
    )


def multicast_y(value):
    half = value.shape[0] // 2
    below = along_y(value, 1)
    above = along_y(value, -1)
    far = [along_y(below[:half], 1), along_y(above[half:], -1)]
    return jnp.concatenate([value, below, above] + far, axis=0)


def reduce_y(value):
    own, below, above, far = jnp.split(value, 4, axis=0)
    half = own.shape[0] // 2
    from_above = along_y(far[:half], -1)
    from_below = along_y(far[half:], 1)
    below = jnp.concatenate([below[:half] + from_above, below[half:]], axis=0)
    above = jnp.concatenate([above[:half], above[half:] + from_below], axis=0)
    parts = [own, along_y(below, -1), along_y(above, 1)]
    return sum(p.astype(F32) for p in parts).astype(BF)


def exchange_z(value, sign):
    parts = jnp.split(value, 4, axis=0)
    return jnp.concatenate(
        [parts[0]] + [along_z(parts[k], sign * k) for k in (1, 2, 3)], axis=0
    )


def per_device(
    tokens, cotangent, node_routes, home_local, second_local, gate_weights, gate_w, up_w, down_w
):
    tok, width = tokens.shape
    half = width // 2
    top = gate_weights.shape[1]
    cap = 5
    nodes = lax.axis_size("node")
    experts = nodes * 4
    node = lax.axis_index("node")
    local = lax.axis_index("local")
    x_pos, z_pos = node // 4, node % 4
    y_pos = local // 2
    first = local % 2 == 0

    lane = jnp.arange(nodes, dtype=jnp.int32)
    node_match = node_routes[:, :, None] == lane[None, None, :]
    home = jnp.sum(jnp.where(node_match, home_local[0][None, None, :], 0), axis=2)
    other = jnp.where(second_local == 0, (home + 1) % 4, (home + second_local) % 4)
    pick = jnp.stack([home, other], axis=2).reshape(tok, top)
    ids = jnp.repeat(node_routes, 2, axis=1) * 4 + pick
    tail_lane = jnp.arange(TAIL, dtype=jnp.int32)
    onehot = ids[:, :, None] == tail_lane[None, None, :]
    tail = jnp.sum(
        jnp.where(onehot, gate_weights.astype(F32)[:, :, None], 0.0), axis=1
    ).astype(BF)

    def chip_rows(array, with_tail):
        left, right = array[:, :half], array[:, half:]
        if with_tail:
            left = jnp.concatenate([left, tail], axis=1)
            right = jnp.concatenate([right, tail], axis=1)
        mine = jnp.where(first, left, right)
        theirs = across(jnp.where(first, right, left))
        return jnp.concatenate(
            [jnp.where(first, mine, theirs), jnp.where(first, theirs, mine)], axis=0
        )

    tok_rows = multicast_x(chip_rows(tokens, True))
    cot_rows = multicast_x(chip_rows(cotangent, False))

    weights = tok_rows[:, half : half + experts]
    count = tok_rows.shape[0]
    groups = count // tok
    slots = groups * cap
    near = 4 * x_pos + (z_pos + jnp.arange(4, dtype=jnp.int32)) % 4
    in_node = (jnp.arange(experts, dtype=jnp.int32)[:, None] // 4 == near[None, :]).astype(BF)
    member = dot((weights != 0).astype(BF), in_node, ((1,), (0,))) > 0
    row = jnp.arange(count, dtype=jnp.int32)
    before = (row[:, None] // tok == row[None, :] // tok) & (row[:, None] > row[None, :])
    rank = dot(before.astype(BF), member.astype(BF), ((1,), (0,))).astype(jnp.int32)
    place = (row // tok * cap)[:, None] + rank
    place = jnp.where(member, place, -1)
    select = (
        (place.T[:, None, :] == jnp.arange(slots, dtype=jnp.int32)[None, :, None])
        .astype(BF)
        .reshape(4 * slots, count)
    )
    tok_slots = dot(select, tok_rows, ((1,), (0,))).astype(BF)
    cot_slots = dot(select, cot_rows, ((1,), (0,))).astype(BF)

    x_own = multicast_y(exchange_z(tok_slots, 1))
    d_own = multicast_y(exchange_z(cot_slots, 1))
    x_tail = x_own[:, half:]
    x_own = x_own[:, :half]
    x_oth = across(x_own)
    d_oth = across(d_own)
    x_left, x_right = jnp.where(first, x_own, x_oth), jnp.where(first, x_oth, x_own)
    d_left, d_right = jnp.where(first, d_own, d_oth), jnp.where(first, d_oth, d_own)

    my_lane = tail_lane == 4 * node + y_pos
    weight = jnp.sum(jnp.where(my_lane[None, :], x_tail.astype(F32), 0.0), axis=1)[:, None]

    gate_proj, up_proj, down_proj = gate_w[0], up_w[0], down_w[0]
    pre_gate = dot(x_left, gate_proj[:half], ((1,), (0,))) + dot(
        x_right, gate_proj[half:], ((1,), (0,))
    )
    pre_up = dot(x_left, up_proj[:half], ((1,), (0,))) + dot(x_right, up_proj[half:], ((1,), (0,)))
    activated, slope = silu_parts(pre_gate)
    hidden = (activated * pre_up).astype(BF)
    hidden_grad = dot(d_left, down_proj[:, :half], ((1,), (1,))) + dot(
        d_right, down_proj[:, half:], ((1,), (1,))
    )
    router = jnp.sum(hidden_grad * hidden.astype(F32), axis=1)[:, None]
    weighted = weight * hidden_grad
    gate_grad = (weighted * pre_up * slope).astype(BF)
    up_grad = (weighted * activated).astype(BF)
    scaled = (weight * hidden.astype(F32)).astype(BF)

    def input_part(rows):
        return dot(gate_grad, gate_proj[rows], ((1,), (1,))) + dot(
            up_grad, up_proj[rows], ((1,), (1,))
        )

    part_left, part_right = input_part(slice(0, half)), input_part(slice(half, width))
    keep = jnp.where(first, part_left, part_right)
    send = jnp.where(first, part_right, part_left).astype(BF)
    router = jnp.where(weight != 0, router, 0.0)

    def router_tail(value):
        high = value.astype(BF)
        low = (value - high.astype(F32)).astype(BF)
        spread = jnp.where(my_lane[None, :], high, jnp.zeros((), BF))
        low_lane = tail_lane == 4 * node + y_pos + TAIL // 2
        return jnp.where(low_lane[None, :], low, spread)

    got = across(jnp.concatenate([send, router_tail(router)], axis=1))
    router = router + jnp.sum(got[:, half:].astype(F32), axis=1)[:, None]
    full = jnp.concatenate(
        [(keep + got[:, :half].astype(F32)).astype(BF), router_tail(router)], axis=1
    )

    returned = exchange_z(reduce_y(full), -1)
    mine, below, above, far = jnp.split(dot(select, returned, ((0,), (0,))).astype(BF), 4, axis=0)
    parts = [mine, along_x(below, -1), along_x(above, 1), along_x(far, 2)]
    chip = sum(p.astype(F32) for p in parts)
    lower, upper = chip[:tok], chip[tok:]
    mine = jnp.where(first, lower, upper)
    theirs = across(jnp.where(first, upper, lower)[:, :half].astype(BF))
    mine_cols = mine[:, :half].astype(BF)
    d_tokens = jnp.concatenate(
        [jnp.where(first, mine_cols, theirs), jnp.where(first, theirs, mine_cols)], axis=1
    )
    by_expert = mine[:, half : half + TAIL // 2] + mine[:, half + TAIL // 2 :]
    by_expert = jnp.concatenate([by_expert, jnp.zeros_like(by_expert)], axis=1)
    d_gates = jnp.sum(jnp.where(onehot, by_expert[:, None, :], 0.0), axis=2).astype(BF)

    down_update = jnp.concatenate(
        [dot(scaled, d_left, ((0,), (0,))).astype(BF), dot(scaled, d_right, ((0,), (0,))).astype(BF)],
        axis=1,
    )

    def projection_update(grad):
        return jnp.concatenate(
            [dot(x_left, grad, ((0,), (0,))).astype(BF), dot(x_right, grad, ((0,), (0,))).astype(BF)],
            axis=0,
        )

    return (
        d_tokens,
        d_gates,
        projection_update(gate_grad)[None],
        projection_update(up_grad)[None],
        down_update[None],
    )


def solution(mesh):
    rows = P(("node", "local"), None)
    blocks = P(("node", "local"), None, None)
    return jax.shard_map(
        per_device,
        mesh=mesh,
        in_specs=(rows,) * 6 + (blocks,) * 3,
        out_specs=(rows, rows, blocks, blocks, blocks),
        check_vma=False,
    )
```

```python
import jax
import jax.numpy as jnp
from jax import lax
from jax.experimental import pallas as pl
from jax.experimental.pallas import tpu as pltpu
from jax.sharding import PartitionSpec as P

BF = jnp.bfloat16
F32 = jnp.float32
TAIL = 128


def along_x(value, step):
    pairs = [(x * 4 + z, (x + step) % 4 * 4 + z) for x in range(4) for z in range(4)]
    return lax.ppermute(value, "node", pairs)


def along_z(value, step):
    pairs = [(x * 4 + z, x * 4 + (z + step) % 4) for x in range(4) for z in range(4)]
    return lax.ppermute(value, "node", pairs)


def along_y(value, step):
    pairs = [(y * 2 + c, (y + step) % 4 * 2 + c) for y in range(4) for c in range(2)]
    return lax.ppermute(value, "local", pairs)


def across(value):
    return lax.ppermute(value, "local", [(i, i ^ 1) for i in range(8)])


def dot(left, right, dims):
    return lax.dot_general(left, right, ((dims[0], dims[1]), ((), ())), preferred_element_type=F32)


def silu_parts(pre_gate):
    sigmoid = jax.nn.sigmoid(pre_gate)
    return (pre_gate * sigmoid, sigmoid * (1.0 + pre_gate * (1.0 - sigmoid)))


def after(value, done):
    return lax.optimization_barrier((value, done))[0]


def multicast_x(value):
    return [value, along_x(value, 1), along_x(value, -1), along_x(value, 2)]


def exchange_z(parts, sign):
    return [parts[0]] + [along_z(parts[k], sign * k) for k in (1, 2, 3)]


def reduce_y(own, below, above, far):
    half = own.shape[0] // 2
    from_above = along_y(far[:half], -1)
    from_below = along_y(far[half:], 1)
    got_early = [along_y(below[half:], -1), along_y(above[:half], 1)]
    got_late = [along_y(below[:half] + from_above, -1), along_y(above[half:] + from_below, 1)]
    top = [own[:half], got_late[0], got_early[1]]
    bottom = [own[half:], got_early[0], got_late[1]]
    add = lambda parts: sum(p.astype(F32) for p in parts).astype(BF)
    return jnp.concatenate([add(top), add(bottom)], axis=0)


def vmem(count):
    return [pl.BlockSpec(memory_space=pltpu.VMEM)] * count


def smem():
    return [pl.BlockSpec(memory_space=pltpu.SMEM)]


def call(kernel, scalars, arrays, outs):
    return pl.pallas_call(
        kernel,
        out_shape=[jax.ShapeDtypeStruct(shape, kind) for shape, kind in outs],
        in_specs=smem() + vmem(len(arrays)),
        out_specs=vmem(len(outs)),
        compiler_params=pltpu.CompilerParams(vmem_limit_bytes=48 * 1024 * 1024),
    )(scalars, *arrays)


def start_kernel(pos, tok, cot, routes, homes, second, weights, tok_keep, tok_send, cot_keep, cot_send):
    rows, width = tok.shape
    half = width // 2
    core = pos[0]
    lane = lax.broadcasted_iota(jnp.int32, (rows, TAIL), 1)
    home_lane = lax.broadcasted_iota(jnp.int32, (rows, homes.shape[1]), 1)
    tail = jnp.zeros((rows, TAIL), F32)
    for j in range(routes.shape[1]):
        node = routes[:, j : j + 1]
        home = jnp.sum(jnp.where(home_lane == node, homes[...], 0), axis=1, keepdims=True)
        other = lax.rem(home + jnp.maximum(second[:, j : j + 1], 1), 4)
        for k, pick in ((2 * j, home), (2 * j + 1, other)):
            weight = weights[:, k : k + 1].astype(F32)
            tail = tail + jnp.where(lane == node * 4 + pick, weight, 0.0)
    tail = tail.astype(BF)
    tok_keep[:, :half] = jnp.where(core == 0, tok[:, :half], tok[:, half:])
    tok_keep[:, half:] = tail
    tok_send[:, :half] = jnp.where(core == 0, tok[:, half:], tok[:, :half])
    tok_send[:, half:] = tail
    cot_keep[...] = jnp.where(core == 0, cot[:, :half], cot[:, half:])
    cot_send[...] = jnp.where(core == 0, cot[:, half:], cot[:, :half])


def nn(left, right):
    return dot(left, right, ((1,), (0,)))


def nt(left, right):
    return dot(left, right, ((1,), (1,)))


def forward_kernel(pos, x_own, x_oth, weight, gate, up, for_gate, for_up, hidden, scaled):
    half = x_own.shape[1]
    mine = pl.ds(pl.multiple_of(pos[0] * half, half), half)
    theirs = pl.ds(pl.multiple_of((1 - pos[0]) * half, half), half)
    width = gate.shape[1]
    step = min(256, width)
    for start in range(0, width, step):
        cols = slice(start, start + step)
        pre_gate = nn(x_own[...], gate[mine, cols]) + nn(x_oth[...], gate[theirs, cols])
        pre_up = nn(x_own[...], up[mine, cols]) + nn(x_oth[...], up[theirs, cols])
        activated, slope = silu_parts(pre_gate)
        hid = (activated * pre_up).astype(BF)
        hidden[:, cols] = hid
        scaled[:, cols] = (weight[...] * hid.astype(F32)).astype(BF)
        for_gate[:, cols] = weight[...] * (pre_up * slope)
        for_up[:, cols] = weight[...] * activated


def router_tail(value, lane, expert):
    high = value.astype(BF).astype(F32)
    return jnp.where(lane == expert, high, 0.0) + jnp.where(
        lane == expert + TAIL // 2, value - high, 0.0
    )


def backward_kernel(
    pos, d_own, d_oth, for_gate, for_up, hidden, weight, gate, up, down, gate_grad, up_grad, router, send
):
    half = d_own.shape[1]
    mine = pl.ds(pl.multiple_of(pos[0] * half, half), half)
    theirs = pl.ds(pl.multiple_of((1 - pos[0]) * half, half), half)
    width = hidden.shape[1]
    step = min(256, width)
    total = jnp.zeros(weight.shape, F32)
    for start in range(0, width, step):
        cols = slice(start, start + step)
        grad = nt(d_own[...], down[cols, mine]) + nt(d_oth[...], down[cols, theirs])
        total = total + jnp.sum(grad * hidden[:, cols].astype(F32), axis=1, keepdims=True)
        gate_grad[:, cols] = (grad * for_gate[:, cols]).astype(BF)
        up_grad[:, cols] = (grad * for_up[:, cols]).astype(BF)
    total = jnp.where(weight[...] != 0, total, 0.0)
    router[...] = total
    step = half // 7 if half % 7 == 0 else half
    for start in range(0, half, step):
        rows = pl.ds(pl.multiple_of((1 - pos[0]) * half + start, step), step)
        part = nt(gate_grad[...], gate[rows, :]) + nt(up_grad[...], up[rows, :])
        send[:, start : start + step] = part.astype(BF)
    lane = lax.broadcasted_iota(jnp.int32, (d_own.shape[0], TAIL), 1)
    send[:, half:] = router_tail(total, lane, pos[1]).astype(BF)


def keep_kernel(pos, gate_grad, up_grad, gate, up, keep):
    half = keep.shape[1]
    step = half // 7 if half % 7 == 0 else half
    for start in range(0, half, step):
        rows = pl.ds(pl.multiple_of(pos[0] * half + start, step), step)
        keep[:, start : start + step] = nt(gate_grad[...], gate[rows, :]) + nt(
            up_grad[...], up[rows, :]
        )


def per_device(
    tokens, cotangent, node_routes, home_local, second_local, gate_weights, gate_w, up_w, down_w
):
    tok, width = tokens.shape
    half = width // 2
    hid_width = gate_w.shape[2]
    top = gate_weights.shape[1]
    cap = 5
    experts = lax.axis_size("node") * 4
    node = lax.axis_index("node")
    local = lax.axis_index("local")
    x_pos, z_pos = node // 4, node % 4
    core = local % 2
    first = core == 0
    my_expert = 4 * node + local // 2
    pos = jnp.stack([core, my_expert]).astype(jnp.int32)

    tok_keep, tok_send, cot_keep, cot_send = call(
        start_kernel,
        pos,
        [tokens, cotangent, node_routes, home_local, second_local, gate_weights],
        [((tok, half + TAIL), BF)] * 2 + [((tok, half), BF)] * 2,
    )
    tok_chip = jnp.concatenate([tok_keep, across(tok_send)], axis=0)
    cot_chip = jnp.concatenate([cot_keep, across(cot_send)], axis=0)
    tok_rows = jnp.concatenate(multicast_x(tok_chip), axis=0)

    weights = tok_rows[:, half : half + experts]
    count = tok_rows.shape[0]
    groups = count // tok
    slots = groups * cap
    near = 4 * x_pos + (z_pos + jnp.arange(4, dtype=jnp.int32)) % 4
    in_node = (jnp.arange(experts, dtype=jnp.int32)[:, None] // 4 == near[None, :]).astype(BF)
    member = nn((weights != 0).astype(BF), in_node) > 0
    row = jnp.arange(count, dtype=jnp.int32)
    before = (row[:, None] // tok == row[None, :] // tok) & (row[:, None] > row[None, :])
    rank = nn(before.astype(BF), member.astype(BF)).astype(jnp.int32)
    group = row // tok
    place = ((group // 2 * 2 + (group + core) % 2) * cap)[:, None] + rank
    place = jnp.where(member, place, -1)
    select = (
        (place.T[:, None, :] == jnp.arange(slots, dtype=jnp.int32)[None, :, None])
        .astype(BF)
        .reshape(4 * slots, count)
    )

    def slot_parts(rows):
        return jnp.split(nn(select, rows).astype(BF), 4, axis=0)

    x_slots = jnp.concatenate(exchange_z(slot_parts(tok_rows), 1), axis=0)
    side = slots * 2
    x_below, x_above = along_y(x_slots, 1), along_y(x_slots, -1)
    x_far = [along_y(x_below[:side], 1), along_y(x_above[side:], -1)]

    cot_rows = jnp.concatenate(multicast_x(after(cot_chip, tok_rows)), axis=0)
    d_parts = after(slot_parts(cot_rows), x_slots)
    d_slots = after(jnp.concatenate(exchange_z(d_parts, 1), axis=0), (x_below, x_above))
    d_below, d_above = along_y(d_slots, 1), along_y(d_slots, -1)
    d_far = [along_y(d_below[:side], 1), along_y(d_above[side:], -1)]

    x_own = jnp.concatenate([x_slots, x_below, x_above] + x_far, axis=0)
    x_tail = x_own[:, half:]
    x_own = x_own[:, :half]
    x_oth = across(x_own)
    d_near = jnp.concatenate([d_slots, d_below, d_above], axis=0)
    d_far = jnp.concatenate(d_far, axis=0)
    d_own = jnp.concatenate([d_near, d_far], axis=0)
    d_oth = jnp.concatenate([across(d_near), across(d_far)], axis=0)

    tail_lane = jnp.arange(TAIL, dtype=jnp.int32)
    my_lane = tail_lane == my_expert
    weight = jnp.sum(jnp.where(my_lane[None, :], x_tail.astype(F32), 0.0), axis=1)[:, None]

    gate_proj, up_proj, down_proj = gate_w[0], up_w[0], down_w[0]
    count = x_own.shape[0]
    for_gate, for_up, hidden, scaled = call(
        forward_kernel,
        pos,
        [x_own, x_oth, weight, gate_proj, up_proj],
        [((count, hid_width), F32)] * 2 + [((count, hid_width), BF)] * 2,
    )
    gate_grad, up_grad, router, send = call(
        backward_kernel,
        pos,
        [d_own, d_oth, for_gate, for_up, hidden, weight, gate_proj, up_proj, down_proj],
        [((count, hid_width), BF)] * 2 + [((count, 1), F32), ((count, half + TAIL), BF)],
    )
    got = across(send)
    keep = call(
        keep_kernel, pos, [gate_grad, up_grad, gate_proj, up_proj], [((count, half), F32)]
    )[0]
    router = router + jnp.sum(got[:, half:].astype(F32), axis=1)[:, None]
    spread = router_tail(router, tail_lane[None, :], my_expert)
    full = jnp.concatenate([keep + got[:, :half].astype(F32), spread], axis=1).astype(BF)

    quarter = count // 4
    returned = reduce_y(*[full[i * quarter : (i + 1) * quarter] for i in range(4)])
    returned = jnp.concatenate(
        exchange_z([returned[i * slots : (i + 1) * slots] for i in range(4)], -1), axis=0
    )
    parts = jnp.split(dot(select, returned, ((0,), (0,))).astype(BF), 4, axis=0)
    parts = [parts[0], along_x(parts[1], -1), along_x(parts[2], 1), along_x(parts[3], 2)]
    chip = sum(p.astype(F32) for p in parts)
    theirs = across(chip[tok:, :half].astype(BF))
    mine = chip[:tok]
    mine_cols = mine[:, :half].astype(BF)
    d_tokens = jnp.concatenate(
        [jnp.where(first, mine_cols, theirs), jnp.where(first, theirs, mine_cols)], axis=1
    )
    by_expert = mine[:, half : half + TAIL // 2] + mine[:, half + TAIL // 2 :]
    by_expert = jnp.concatenate([by_expert, jnp.zeros_like(by_expert)], axis=1)
    lane16 = jnp.arange(home_local.shape[1], dtype=jnp.int32)
    node_match = node_routes[:, :, None] == lane16[None, None, :]
    home = jnp.sum(jnp.where(node_match, home_local[0][None, None, :], 0), axis=2)
    other = (home + jnp.maximum(second_local, 1)) % 4
    pick = jnp.stack([home, other], axis=2).reshape(tok, top)
    ids = jnp.repeat(node_routes, 2, axis=1) * 4 + pick
    onehot = ids[:, :, None] == tail_lane[None, None, :]
    d_gates = jnp.sum(jnp.where(onehot, by_expert[:, None, :], 0.0), axis=2).astype(BF)

    x_own, x_oth, d_own, d_oth, gate_grad, up_grad, scaled = after(
        (x_own, x_oth, d_own, d_oth, gate_grad, up_grad, scaled), full
    )
    x_left, x_right = jnp.where(first, x_own, x_oth), jnp.where(first, x_oth, x_own)
    d_left, d_right = jnp.where(first, d_own, d_oth), jnp.where(first, d_oth, d_own)

    def update(left, right):
        return dot(left, right, ((0,), (0,))).astype(BF)

    down_update = jnp.concatenate([update(scaled, d_left), update(scaled, d_right)], axis=1)

    def projection_update(grad):
        return jnp.concatenate([update(x_left, grad), update(x_right, grad)], axis=0)

    return (
        d_tokens,
        d_gates,
        projection_update(gate_grad)[None],
        projection_update(up_grad)[None],
        down_update[None],
    )


def solution(mesh):
    rows = P(("node", "local"), None)
    blocks = P(("node", "local"), None, None)
    return jax.shard_map(
        per_device,
        mesh=mesh,
        in_specs=(rows,) * 6 + (blocks,) * 3,
        out_specs=(rows, rows, blocks, blocks, blocks),
        check_vma=False,
    )
```

```python
import jax
import jax.numpy as jnp
from jax import lax
from jax.experimental import pallas as pl
from jax.experimental.pallas import tpu as pltpu
from jax.sharding import PartitionSpec as P

BF = jnp.bfloat16
F32 = jnp.float32
TAIL = 128


def along_x(value, step):
    pairs = [(x * 4 + z, (x + step) % 4 * 4 + z) for x in range(4) for z in range(4)]
    return lax.ppermute(value, "node", pairs)


def along_z(value, step):
    pairs = [(x * 4 + z, x * 4 + (z + step) % 4) for x in range(4) for z in range(4)]
    return lax.ppermute(value, "node", pairs)


def along_y(value, step):
    pairs = [(y * 2 + c, (y + step) % 4 * 2 + c) for y in range(4) for c in range(2)]
    return lax.ppermute(value, "local", pairs)


def across(value):
    return lax.ppermute(value, "local", [(i, i ^ 1) for i in range(8)])


def dot(left, right, dims):
    return lax.dot_general(left, right, ((dims[0], dims[1]), ((), ())), preferred_element_type=F32)


def silu_parts(pre_gate):
    sigmoid = jax.nn.sigmoid(pre_gate)
    return (pre_gate * sigmoid, sigmoid * (1.0 + pre_gate * (1.0 - sigmoid)))


def exchange_z(parts, sign):
    return [parts[0]] + [along_z(parts[k], sign * k) for k in (1, 2, 3)]


def nn(left, right):
    return dot(left, right, ((1,), (0,)))


def nt(left, right):
    return dot(left, right, ((1,), (1,)))


def tn(left, right):
    return dot(left, right, ((0,), (0,)))


def vmem(count):
    return [pl.BlockSpec(memory_space=pltpu.VMEM)] * count


def start_kernel(core, tok, cot, routes, homes, second, weights, keep, send):
    rows, width = tok.shape
    half = width // 2
    nodes = homes.shape[1]
    first = core[0] == 0
    lane = lax.broadcasted_iota(jnp.int32, (TAIL, rows), 0)
    row_id = lax.broadcasted_iota(jnp.int32, (nodes, nodes), 0)
    col_id = lax.broadcasted_iota(jnp.int32, (nodes, nodes), 1)
    home_col = jnp.sum(jnp.where(row_id == col_id, homes[...], 0), axis=1, keepdims=True)
    node_id = lax.broadcasted_iota(jnp.int32, (nodes, rows), 0)
    tail = jnp.zeros((TAIL, rows), F32)
    for j in range(routes.shape[0]):
        node = routes[j : j + 1, :]
        home = jnp.sum(jnp.where(node_id == node, home_col, 0), axis=0, keepdims=True)
        other = lax.rem(home + jnp.maximum(second[j : j + 1, :], 1), 4)
        for k, pick in ((2 * j, home), (2 * j + 1, other)):
            weight = weights[k : k + 1, :].astype(F32)
            tail = tail + jnp.where(lane == node * 4 + pick, weight, 0.0)
    tail = tail.T.astype(BF)
    for out, is_left in ((keep, first), (send, jnp.logical_not(first))):
        out[:, :half] = jnp.where(is_left, tok[:, :half], tok[:, half:])
        out[:, half : half + TAIL] = tail
        out[:, half + TAIL :] = jnp.where(is_left, cot[:, :half], cot[:, half:])


def gate_kernel(pre_gate, pre_up, weight, hidden, scaled, for_gate, for_up):
    activated, slope = silu_parts(pre_gate[...])
    hid = (activated * pre_up[...]).astype(BF)
    hidden[...] = hid
    scaled[...] = (weight[...] * hid.astype(F32)).astype(BF)
    for_gate[...] = weight[...] * (pre_up[...] * slope)
    for_up[...] = weight[...] * activated


def join_kernel(expert, keep, got, router, *outs):
    half = keep.shape[1]
    step = outs[0].shape[0]
    got_tail = got[:, half:].astype(F32)
    total = router[...] + jnp.sum(got_tail, axis=1, keepdims=True)
    lane = lax.broadcasted_iota(jnp.int32, got_tail.shape, 1)
    high = total.astype(BF).astype(F32)
    tail = jnp.where(lane == expert[0], high, 0.0)
    tail = jnp.where(lane == expert[0] + TAIL // 2, total - high, tail).astype(BF)
    for i, out in enumerate(outs):
        rows = slice(i * step, (i + 1) * step)
        out[:, :half] = (keep[rows, :] + got[rows, :half].astype(F32)).astype(BF)
        out[:, half:] = tail[rows, :]


def per_device(
    tokens, cotangent, node_routes, home_local, second_local, gate_weights, gate_w, up_w, down_w
):
    tok, width = tokens.shape
    half = width // 2
    top = gate_weights.shape[1]
    cap = 5
    experts = lax.axis_size("node") * 4
    node = lax.axis_index("node")
    local = lax.axis_index("local")
    x_pos, z_pos = node // 4, node % 4
    core = local % 2
    first = core == 0
    my_expert = 4 * node + local // 2
    never = core > 1

    def hold(value, *done):
        for d in done:
            corner = lax.slice(d, (0, 0), (1, 1)).astype(value.dtype)
            value = jnp.where(never, corner, value)
        return value

    raw_keep, raw_send = pl.pallas_call(
        start_kernel,
        out_shape=[jax.ShapeDtypeStruct((tok, width + TAIL), BF)] * 2,
        in_specs=[pl.BlockSpec(memory_space=pltpu.SMEM)] + [pl.BlockSpec()] * 6,
        out_specs=vmem(2),
    )(
        core.astype(jnp.int32).reshape(1),
        tokens,
        cotangent,
        node_routes.T,
        home_local,
        second_local.T,
        gate_weights.T,
    )
    chip = jnp.concatenate([raw_keep, across(raw_send)], axis=0)
    rows = jnp.concatenate(
        [chip, along_x(chip, 1), along_x(chip, -1), along_x(chip, 2)], axis=0
    )

    weights = rows[:, half : half + experts]
    count = rows.shape[0]
    groups = count // tok
    slots = groups * cap
    nearby = 4 * x_pos + (z_pos + jnp.arange(4, dtype=jnp.int32)) % 4
    in_node = (jnp.arange(experts, dtype=jnp.int32)[:, None] // 4 == nearby[None, :]).astype(BF)
    member = nn((weights != 0).astype(BF), in_node) > 0
    row = jnp.arange(count, dtype=jnp.int32)
    before = (row[:, None] // tok == row[None, :] // tok) & (row[:, None] > row[None, :])
    rank = nn(before.astype(BF), member.astype(BF)).astype(jnp.int32)
    group = row // tok
    place = ((group // 2 * 2 + (group + core) % 2) * cap)[:, None] + rank
    place = jnp.where(member, place, -1)
    select = (
        (place.T[:, None, :] == jnp.arange(slots, dtype=jnp.int32)[None, :, None])
        .astype(BF)
        .reshape(4 * slots, count)
    )
    x_parts = jnp.split(nn(select, rows[:, : half + TAIL]).astype(BF), 4, axis=0)
    d_parts = jnp.split(nn(select, rows[:, half + TAIL :]).astype(BF), 4, axis=0)
    side = 2 * slots

    def both_ways(mine):
        return along_y(mine, 1), along_y(mine, -1)

    def far_of(below, above):
        return jnp.concatenate([along_y(below, 1), along_y(above, -1)], axis=0)

    def whole(mine, theirs):
        return jnp.where(
            first,
            jnp.concatenate([mine, theirs], axis=1),
            jnp.concatenate([theirs, mine], axis=1),
        )

    gate_proj, up_proj, down_proj = gate_w[0], up_w[0], down_w[0]

    def pick(array, which):
        return lax.dynamic_slice_in_dim(array, which * half, half, 0)

    gate_own, gate_oth = pick(gate_proj, core), pick(gate_proj, 1 - core)
    up_own, up_oth = pick(up_proj, core), pick(up_proj, 1 - core)
    tail_lane = jnp.arange(TAIL, dtype=jnp.int32)[None, :]

    def forward(rows, *done):
        mine = rows[:, :half]
        x = hold(whole(mine, across(mine)), *done)
        weight = jnp.sum(
            jnp.where(tail_lane == my_expert, rows[:, half:].astype(F32), 0.0),
            axis=1,
            keepdims=True,
        )
        pre_gate = nn(x, gate_proj)
        pre_up = nn(x, up_proj)
        shape = pre_gate.shape
        return [x, weight] + list(pl.pallas_call(
            gate_kernel,
            out_shape=[jax.ShapeDtypeStruct(shape, kind) for kind in (BF, BF, F32, F32)],
            in_specs=vmem(3),
            out_specs=vmem(4),
        )(pre_gate, pre_up, weight))

    def backward(d, state):
        x, weight, hidden, scaled, for_gate, for_up = state
        hidden_grad = nt(d, down_proj)
        router = jnp.sum(hidden_grad * hidden.astype(F32), axis=1, keepdims=True)
        router = jnp.where(weight != 0, router, 0.0)
        dg = (hidden_grad * for_gate).astype(BF)
        du = (hidden_grad * for_up).astype(BF)
        send = (nt(dg, gate_oth) + nt(du, up_oth)).astype(BF)
        high = router.astype(BF)
        low = (router - high.astype(F32)).astype(BF)
        tail = jnp.where(tail_lane == my_expert, high, jnp.zeros((), BF))
        tail = jnp.where(tail_lane == my_expert + TAIL // 2, low, tail)
        return dg, du, router, jnp.concatenate([send, tail], axis=1)

    def join(dg, du, router, send, *done):
        got = across(send)
        keep = nt(hold(dg, send, *done), gate_own) + nt(hold(du, send, *done), up_own)
        pieces = dg.shape[0] // side
        return pl.pallas_call(
            join_kernel,
            out_shape=[jax.ShapeDtypeStruct((side, half + TAIL), BF)] * pieces,
            in_specs=[pl.BlockSpec(memory_space=pltpu.SMEM)] + vmem(3),
            out_specs=vmem(pieces),
        )(my_expert.astype(jnp.int32).reshape(1), keep, got, router)

    x_parts = exchange_z(x_parts, 1)
    x_slots = jnp.concatenate(x_parts, axis=0)
    x_below, x_above = both_ways(x_slots)
    d_parts = [hold(part, *x_parts[1:]) for part in d_parts]
    d_slots = jnp.concatenate(exchange_z(d_parts, 1), axis=0)
    d_below, d_above = both_ways(d_slots)
    x_far = far_of(x_below[:side], x_above[side:])
    near_state = forward(jnp.concatenate([x_slots, x_below, x_above], axis=0))
    d_far = far_of(hold(d_below[:side], near_state[4]), hold(d_above[side:], near_state[4]))
    far_state = forward(x_far, near_state[4])
    d_near = jnp.concatenate([d_slots, d_below, d_above], axis=0)
    d_near = hold(whole(d_near, across(d_near)), far_state[4])
    near = backward(d_near, near_state)
    d_far = hold(whole(d_far, across(d_far)), near[3])
    far = backward(d_far, far_state)
    joined = [join(*near)]
    joined.append(join(*far, joined[0][0]))

    own_top, own_bottom, below_top, below_bottom, above_top, above_bottom = joined[0]
    far_top, far_bottom = joined[1]
    from_above = along_y(far_top, -1)
    from_below = along_y(far_bottom, 1)
    early_top, early_bottom = along_y(above_top, 1), along_y(below_bottom, -1)
    late_top = along_y(below_top + from_above, -1)
    late_bottom = along_y(above_bottom + from_below, 1)

    def add(*parts):
        return sum(p.astype(F32) for p in parts).astype(BF)

    top_rows = add(own_top, early_top, late_top)
    bottom_rows = add(own_bottom, early_bottom, late_bottom)
    back = [top_rows[:slots], top_rows[slots:], bottom_rows[:slots], bottom_rows[slots:]]
    back = jnp.concatenate(exchange_z(back, -1), axis=0)
    parts = jnp.split(tn(select, back).astype(BF), 4, axis=0)
    parts = [parts[0], along_x(parts[1], -1), along_x(parts[2], 1), along_x(parts[3], 2)]
    chip = sum(p.astype(F32) for p in parts)
    theirs = across(chip[tok:, :half].astype(BF))
    mine = chip[:tok]
    mine_cols = mine[:, :half].astype(BF)
    d_tokens = jnp.concatenate(
        [jnp.where(first, mine_cols, theirs), jnp.where(first, theirs, mine_cols)], axis=1
    )
    by_expert = mine[:, half : half + TAIL // 2] + mine[:, half + TAIL // 2 :]
    by_expert = jnp.concatenate([by_expert, jnp.zeros_like(by_expert)], axis=1)
    lane16 = jnp.arange(home_local.shape[1], dtype=jnp.int32)
    node_match = node_routes[:, :, None] == lane16[None, None, :]
    home = jnp.sum(jnp.where(node_match, home_local[0][None, None, :], 0), axis=2)
    other = (home + jnp.maximum(second_local, 1)) % 4
    ids = jnp.repeat(node_routes, 2, axis=1) * 4 + jnp.stack([home, other], axis=2).reshape(tok, top)
    onehot = ids[:, :, None] == tail_lane[None, :, :]
    d_gates = jnp.sum(jnp.where(onehot, by_expert[:, None, :], 0.0), axis=2).astype(BF)

    def rows_of(one, two):
        return hold(jnp.concatenate([one, two], axis=0), joined[1][0])

    x_rows = rows_of(near_state[0], far_state[0])
    d_rows = rows_of(d_near, d_far)
    gate_grad, up_grad = rows_of(near[0], far[0]), rows_of(near[1], far[1])
    scaled = rows_of(near_state[3], far_state[3])
    return (
        d_tokens,
        d_gates,
        tn(x_rows, gate_grad).astype(BF)[None],
        tn(x_rows, up_grad).astype(BF)[None],
        tn(scaled, d_rows).astype(BF)[None],
    )


def solution(mesh):
    rows = P(("node", "local"), None)
    blocks = P(("node", "local"), None, None)
    return jax.shard_map(
        per_device,
        mesh=mesh,
        in_specs=(rows,) * 6 + (blocks,) * 3,
        out_specs=(rows, rows, blocks, blocks, blocks),
        check_vma=False,
    )
```

```python
import functools

import jax
import jax.numpy as jnp
from jax import lax
from jax.experimental import pallas as pl
from jax.experimental.pallas import tpu as pltpu
from jax.sharding import PartitionSpec as P

BF = jnp.bfloat16
F32 = jnp.float32
TAIL = 128


def along_x(value, step):
    pairs = [(x * 4 + z, (x + step) % 4 * 4 + z) for x in range(4) for z in range(4)]
    return lax.ppermute(value, "node", pairs)


def along_z(value, step):
    pairs = [(x * 4 + z, x * 4 + (z + step) % 4) for x in range(4) for z in range(4)]
    return lax.ppermute(value, "node", pairs)


def along_y(value, step):
    pairs = [(y * 2 + c, (y + step) % 4 * 2 + c) for y in range(4) for c in range(2)]
    return lax.ppermute(value, "local", pairs)


def across(value):
    return lax.ppermute(value, "local", [(i, i ^ 1) for i in range(8)])


def dot(left, right, dims):
    return lax.dot_general(left, right, ((dims[0], dims[1]), ((), ())), preferred_element_type=F32)


def silu_parts(pre_gate):
    sigmoid = jax.nn.sigmoid(pre_gate)
    return (pre_gate * sigmoid, sigmoid * (1.0 + pre_gate * (1.0 - sigmoid)))


def exchange_z(parts, sign):
    return [parts[0]] + [along_z(parts[k], sign * k) for k in (1, 2, 3)]


def nn(left, right):
    return dot(left, right, ((1,), (0,)))


def nt(left, right):
    return dot(left, right, ((1,), (1,)))


def tn(left, right):
    return dot(left, right, ((0,), (0,)))


def vmem(count):
    return [pl.BlockSpec(memory_space=pltpu.VMEM)] * count


def start_kernel(core, tok, cot, routes, homes, second, weights, keep, send):
    rows, width = tok.shape
    half = width // 2
    nodes = homes.shape[1]
    first = core[0] == 0
    lane = lax.broadcasted_iota(jnp.int32, (TAIL, rows), 0)
    row_id = lax.broadcasted_iota(jnp.int32, (nodes, nodes), 0)
    col_id = lax.broadcasted_iota(jnp.int32, (nodes, nodes), 1)
    home_col = jnp.sum(jnp.where(row_id == col_id, homes[...], 0), axis=1, keepdims=True)
    node_id = lax.broadcasted_iota(jnp.int32, (nodes, rows), 0)
    tail = jnp.zeros((TAIL, rows), F32)
    for j in range(routes.shape[0]):
        node = routes[j : j + 1, :]
        home = jnp.sum(jnp.where(node_id == node, home_col, 0), axis=0, keepdims=True)
        other = lax.rem(home + jnp.maximum(second[j : j + 1, :], 1), 4)
        for k, pick in ((2 * j, home), (2 * j + 1, other)):
            weight = weights[k : k + 1, :].astype(F32)
            tail = tail + jnp.where(lane == node * 4 + pick, weight, 0.0)
    tail = tail.T.astype(BF)
    for out, is_left in ((keep, first), (send, jnp.logical_not(first))):
        out[:, :half] = jnp.where(is_left, tok[:, :half], tok[:, half:])
        out[:, half : half + TAIL] = tail
        out[:, half + TAIL :] = jnp.where(is_left, cot[:, :half], cot[:, half:])


def weight_kernel(core, gate, up, _, gate_own, gate_oth, up_own, up_oth, done, sems):
    half = gate.shape[0] // 2
    copies = []
    for src, outs in ((gate, (gate_own, gate_oth)), (up, (up_own, up_oth))):
        for out, which in zip(outs, (core[0], 1 - core[0])):
            rows = pl.ds(pl.multiple_of(which * half, half), half)
            copy = pltpu.make_async_copy(
                src.at[rows, :], out.at[pl.ds(0, half), :], sems.at[len(copies)]
            )
            copies.append(copy)
            copy.start()
    for out in (gate_own, gate_oth, up_own, up_oth):
        out[half:, :] = jnp.zeros((out.shape[0] - half, out.shape[1]), BF)
    done[...] = jnp.zeros(done.shape, F32)
    for copy in copies:
        copy.wait()


def stack_kernel(count, *refs):
    start = 0
    for ref in refs[:count]:
        refs[-1][pl.ds(start, ref.shape[0]), :] = ref[...]
        start += ref.shape[0]


def halves_kernel(below, above, _, below_top, above_bottom):
    side = below_top.shape[0]
    below_top[...] = below[:side, :]
    above_bottom[...] = above[side:, :]


def assemble_kernel(count, pos, *refs):
    refs, outs = refs[: 2 * count], refs[2 * count :]
    half = outs[0].shape[1] // 2
    mine = pl.ds(pl.multiple_of(pos[0] * half, half), half)
    theirs = pl.ds(pl.multiple_of((1 - pos[0]) * half, half), half)
    start = 0
    for own, oth in zip(refs[:count], refs[count:]):
        rows = pl.ds(start, own.shape[0])
        outs[0][rows, mine] = own[:, :half]
        outs[0][rows, theirs] = oth[:, :half]
        if len(outs) > 1:
            tail = own[:, half:].astype(F32)
            lane = lax.broadcasted_iota(jnp.int32, tail.shape, 1)
            outs[1][rows, :] = jnp.sum(
                jnp.where(lane == pos[1], tail, 0.0), axis=1, keepdims=True
            )
        start += own.shape[0]


def pack_kernel(select, rows, *refs):
    outs = refs[-4:]
    packed = nn(select[...], rows[...]).astype(BF)
    step = outs[0].shape[0]
    for i, out in enumerate(outs):
        out[...] = packed[i * step : (i + 1) * step, :]


def per_device(
    tokens, cotangent, node_routes, home_local, second_local, gate_weights, gate_w, up_w, down_w
):
    tok, width = tokens.shape
    half = width // 2
    top = gate_weights.shape[1]
    cap = 5
    experts = lax.axis_size("node") * 4
    node = lax.axis_index("node")
    local = lax.axis_index("local")
    x_pos, z_pos = node // 4, node % 4
    core = local % 2
    first = core == 0
    my_expert = 4 * node + local // 2
    core_arg = core.astype(jnp.int32).reshape(1)
    anywhere = pl.BlockSpec(memory_space=pl.ANY)

    raw_keep, raw_send = pl.pallas_call(
        start_kernel,
        out_shape=[jax.ShapeDtypeStruct((tok, width + TAIL), BF)] * 2,
        in_specs=[pl.BlockSpec(memory_space=pltpu.SMEM)] + [pl.BlockSpec()] * 6,
        out_specs=vmem(2),
    )(
        core_arg,
        tokens,
        cotangent,
        node_routes.T,
        home_local,
        second_local.T,
        gate_weights.T,
    )
    chip = jnp.concatenate([raw_keep, across(raw_send)], axis=0)
    rows = jnp.concatenate(
        [chip, along_x(chip, 1), along_x(chip, -1), along_x(chip, 2)], axis=0
    )

    weights = rows[:, half : half + experts]
    count = rows.shape[0]
    groups = count // tok
    slots = groups * cap
    nearby = 4 * x_pos + (z_pos + jnp.arange(4, dtype=jnp.int32)) % 4
    in_node = (jnp.arange(experts, dtype=jnp.int32)[:, None] // 4 == nearby[None, :]).astype(BF)
    member = nn((weights != 0).astype(BF), in_node) > 0
    row = jnp.arange(count, dtype=jnp.int32)
    before = (row[:, None] // tok == row[None, :] // tok) & (row[:, None] > row[None, :])
    rank = nn(before.astype(BF), member.astype(BF)).astype(jnp.int32)
    group = row // tok
    place = ((group // 2 * 2 + (group + core) % 2) * cap)[:, None] + rank
    place = jnp.where(member, place, -1)
    select = (
        (place.T[:, None, :] == jnp.arange(slots, dtype=jnp.int32)[None, :, None])
        .astype(BF)
        .reshape(4 * slots, count)
    )
    x_parts = jnp.split(nn(select, rows[:, : half + TAIL]).astype(BF), 4, axis=0)
    side = 2 * slots

    hid_width = gate_w.shape[2]
    gate_own, gate_oth, up_own, up_oth, placed = pl.pallas_call(
        weight_kernel,
        out_shape=[jax.ShapeDtypeStruct((half + TAIL, hid_width), BF)] * 4
        + [jax.ShapeDtypeStruct((8, 128), F32)],
        in_specs=[pl.BlockSpec(memory_space=pltpu.SMEM)] + [anywhere] * 3,
        out_specs=vmem(5),
        scratch_shapes=[pltpu.SemaphoreType.DMA((4,))],
    )(core_arg, gate_w[0], up_w[0], raw_send)

    def both_ways(mine):
        return along_y(mine, 1), along_y(mine, -1)

    def far_of(below, above, done):
        below_top, above_bottom = pl.pallas_call(
            halves_kernel,
            out_shape=[jax.ShapeDtypeStruct((side, below.shape[1]), BF)] * 2,
            in_specs=vmem(3),
            out_specs=vmem(2),
        )(below, above, done)
        return [along_y(below_top, 1), along_y(above_bottom, -1)]

    pos = jnp.stack([core, my_expert]).astype(jnp.int32)

    def stack(parts, *done):
        shape = (sum(p.shape[0] for p in parts), parts[0].shape[1])
        return pl.pallas_call(
            functools.partial(stack_kernel, len(parts)),
            out_shape=jax.ShapeDtypeStruct(shape, BF),
            in_specs=vmem(len(parts) + len(done)),
            out_specs=vmem(1)[0],
        )(*parts, *done)

    def both_cores(parts, with_weight):
        count = sum(p.shape[0] for p in parts)
        outs = [jax.ShapeDtypeStruct((count, width), BF)]
        if with_weight:
            outs.append(jax.ShapeDtypeStruct((count, 1), F32))
        return pl.pallas_call(
            functools.partial(assemble_kernel, len(parts)),
            out_shape=outs,
            in_specs=[pl.BlockSpec(memory_space=pltpu.SMEM)] + vmem(2 * len(parts)),
            out_specs=vmem(len(outs)),
        )(pos, *parts, *[across(p) for p in parts])

    x_parts = exchange_z(x_parts, 1)
    x_slots = jnp.concatenate(x_parts, axis=0)
    x_below, x_above = both_ways(x_slots)
    d_parts = pl.pallas_call(
        pack_kernel,
        out_shape=[jax.ShapeDtypeStruct((slots, half), BF)] * 4,
        in_specs=vmem(2) + [anywhere] * 4,
        out_specs=vmem(4),
    )(select, rows[:, half + TAIL :], placed, *x_parts[1:])
    d_slots = jnp.concatenate(exchange_z(d_parts, 1), axis=0)
    d_below, d_above = both_ways(d_slots)
    x_rows = stack([x_slots, x_below, x_above] + far_of(x_below, x_above, d_slots))
    x_all, weight = both_cores([x_rows], True)

    pre_gate = nn(x_all, gate_w[0])
    pre_up = nn(x_all, up_w[0])
    activated, slope = silu_parts(pre_gate)
    hidden = (activated * pre_up).astype(BF)
    scaled = (weight * hidden.astype(F32)).astype(BF)
    hidden, scaled, for_gate, for_up = lax.optimization_barrier(
        (hidden, scaled, weight * (pre_up * slope), weight * activated)
    )
    d_far = stack(far_of(d_below, d_above, d_slots), hidden)
    (d_all,) = both_cores([d_slots, d_below, d_above, d_far], False)
    hidden_grad = nt(d_all, down_w[0])
    gate_grad = (hidden_grad * for_gate).astype(BF)
    up_grad = (hidden_grad * for_up).astype(BF)
    send = (nt(gate_grad, gate_oth) + nt(up_grad, up_oth)).astype(BF)
    got = across(send)
    keep = nt(gate_grad, gate_own) + nt(up_grad, up_own)
    router = jnp.sum(hidden_grad * hidden.astype(F32), axis=1)
    router = jnp.where(weight[:, 0] != 0, router, 0.0)
    router = (router + across(router))[:, None]
    high = router.astype(BF).astype(F32)
    column = jnp.arange(half + TAIL, dtype=jnp.int32)[None, :]
    full = keep + got.astype(F32)
    full = jnp.where(column == half + my_expert, high, full)
    full = jnp.where(column == half + TAIL // 2 + my_expert, router - high, full).astype(BF)
    pieces = lax.optimization_barrier(tuple(jnp.split(full, 8, axis=0)))
    own_top, own_bottom, below_top, below_bottom, above_top, above_bottom = pieces[:6]
    far_top, far_bottom = pieces[6:]
    from_above = along_y(far_top, -1)
    from_below = along_y(far_bottom, 1)
    early_top, early_bottom = along_y(above_top, 1), along_y(below_bottom, -1)
    late_top = along_y(below_top + from_above, -1)
    late_bottom = along_y(above_bottom + from_below, 1)

    def add(*parts):
        return sum(p.astype(F32) for p in parts).astype(BF)

    top_rows = add(own_top, early_top, late_top)
    bottom_rows = add(own_bottom, early_bottom, late_bottom)
    back = [top_rows[:slots], top_rows[slots:], bottom_rows[:slots], bottom_rows[slots:]]
    back = jnp.concatenate(exchange_z(back, -1), axis=0)
    parts = jnp.split(tn(select, back).astype(BF), 4, axis=0)
    parts = [parts[0], along_x(parts[1], -1), along_x(parts[2], 1), along_x(parts[3], 2)]
    chip = sum(p.astype(F32) for p in parts)
    theirs = across(chip[tok:, :half].astype(BF))
    mine = chip[:tok]
    mine_cols = mine[:, :half].astype(BF)
    d_tokens = jnp.concatenate(
        [jnp.where(first, mine_cols, theirs), jnp.where(first, theirs, mine_cols)], axis=1
    )
    by_expert = mine[:, half : half + TAIL // 2] + mine[:, half + TAIL // 2 :]
    by_expert = jnp.concatenate([by_expert, jnp.zeros_like(by_expert)], axis=1)
    lane16 = jnp.arange(home_local.shape[1], dtype=jnp.int32)
    node_match = node_routes[:, :, None] == lane16[None, None, :]
    home = jnp.sum(jnp.where(node_match, home_local[0][None, None, :], 0), axis=2)
    other = (home + jnp.maximum(second_local, 1)) % 4
    ids = jnp.repeat(node_routes, 2, axis=1) * 4 + jnp.stack([home, other], axis=2).reshape(tok, top)
    onehot = ids[:, :, None] == jnp.arange(TAIL, dtype=jnp.int32)[None, None, :]
    d_gates = jnp.sum(jnp.where(onehot, by_expert[:, None, :], 0.0), axis=2).astype(BF)

    return (
        d_tokens,
        d_gates,
        tn(x_all, gate_grad).astype(BF)[None],
        tn(x_all, up_grad).astype(BF)[None],
        tn(scaled, d_all).astype(BF)[None],
    )


def solution(mesh):
    rows = P(("node", "local"), None)
    blocks = P(("node", "local"), None, None)
    return jax.shard_map(
        per_device,
        mesh=mesh,
        in_specs=(rows,) * 6 + (blocks,) * 3,
        out_specs=(rows, rows, blocks, blocks, blocks),
        check_vma=False,
    )
```

```python
import jax
import jax.numpy as jnp
from jax import lax
from jax.experimental import pallas as pl
from jax.experimental.pallas import tpu as pltpu
from jax.sharding import PartitionSpec as P

BF = jnp.bfloat16
F32 = jnp.float32
TAIL = 128


def along_x(value, step):
    pairs = [(x * 4 + z, (x + step) % 4 * 4 + z) for x in range(4) for z in range(4)]
    return lax.ppermute(value, "node", pairs)


def along_z(value, step):
    pairs = [(x * 4 + z, x * 4 + (z + step) % 4) for x in range(4) for z in range(4)]
    return lax.ppermute(value, "node", pairs)


def along_y(value, step):
    pairs = [(y * 2 + c, (y + step) % 4 * 2 + c) for y in range(4) for c in range(2)]
    return lax.ppermute(value, "local", pairs)


def across(value):
    return lax.ppermute(value, "local", [(i, i ^ 1) for i in range(8)])


def dot(left, right, dims):
    return lax.dot_general(left, right, ((dims[0], dims[1]), ((), ())), preferred_element_type=F32)


def silu_parts(pre_gate):
    sigmoid = jax.nn.sigmoid(pre_gate)
    return (pre_gate * sigmoid, sigmoid * (1.0 + pre_gate * (1.0 - sigmoid)))


def exchange_z(parts, sign):
    return [parts[0]] + [along_z(parts[k], sign * k) for k in (1, 2, 3)]


def nn(left, right):
    return dot(left, right, ((1,), (0,)))


def nt(left, right):
    return dot(left, right, ((1,), (1,)))


def tn(left, right):
    return dot(left, right, ((0,), (0,)))


def vmem(count):
    return [pl.BlockSpec(memory_space=pltpu.VMEM)] * count


def start_kernel(core, tok, cot, routes, homes, second, weights, keep, send):
    rows, width = tok.shape
    half = width // 2
    nodes = homes.shape[1]
    first = core[0] == 0
    lane = lax.broadcasted_iota(jnp.int32, (TAIL, rows), 0)
    row_id = lax.broadcasted_iota(jnp.int32, (nodes, nodes), 0)
    col_id = lax.broadcasted_iota(jnp.int32, (nodes, nodes), 1)
    home_col = jnp.sum(jnp.where(row_id == col_id, homes[...], 0), axis=1, keepdims=True)
    node_id = lax.broadcasted_iota(jnp.int32, (nodes, rows), 0)
    tail = jnp.zeros((TAIL, rows), F32)
    for j in range(routes.shape[0]):
        node = routes[j : j + 1, :]
        home = jnp.sum(jnp.where(node_id == node, home_col, 0), axis=0, keepdims=True)
        other = lax.rem(home + jnp.maximum(second[j : j + 1, :], 1), 4)
        for k, pick in ((2 * j, home), (2 * j + 1, other)):
            weight = weights[k : k + 1, :].astype(F32)
            tail = tail + jnp.where(lane == node * 4 + pick, weight, 0.0)
    tail = tail.T.astype(BF)
    for out, is_left in ((keep, first), (send, jnp.logical_not(first))):
        out[:, :half] = jnp.where(is_left, tok[:, :half], tok[:, half:])
        out[:, half : half + TAIL] = tail
        out[:, half + TAIL :] = jnp.where(is_left, cot[:, :half], cot[:, half:])


def weight_kernel(core, gate, up, down, _, gate_own, gate_oth, up_own, up_oth, down_own, down_oth, sems):
    half = down_own.shape[1]
    copies = []
    for src, outs in ((gate, (gate_own, gate_oth)), (up, (up_own, up_oth))):
        for out, which in zip(outs, (core[0], 1 - core[0])):
            rows = pl.ds(pl.multiple_of(which * half, half), half)
            copies.append((src.at[rows, :], out.at[pl.ds(0, half), :]))
    for out, which in ((down_own, core[0]), (down_oth, 1 - core[0])):
        cols = pl.ds(pl.multiple_of(which * half, half), half)
        copies.append((down.at[:, cols], out))
    copies = [
        pltpu.make_async_copy(src, dst, sems.at[i]) for i, (src, dst) in enumerate(copies)
    ]
    for copy in copies:
        copy.start()
    for out in (gate_own, gate_oth, up_own, up_oth):
        out[half:, :] = jnp.zeros((out.shape[0] - half, out.shape[1]), BF)
    for copy in copies:
        copy.wait()


def per_device(
    tokens, cotangent, node_routes, home_local, second_local, gate_weights, gate_w, up_w, down_w
):
    tok, width = tokens.shape
    half = width // 2
    top = gate_weights.shape[1]
    cap = 5
    experts = lax.axis_size("node") * 4
    node = lax.axis_index("node")
    local = lax.axis_index("local")
    x_pos, z_pos = node // 4, node % 4
    core = local % 2
    first = core == 0
    my_expert = 4 * node + local // 2
    core_arg = core.astype(jnp.int32).reshape(1)
    anywhere = pl.BlockSpec(memory_space=pl.ANY)

    raw_keep, raw_send = pl.pallas_call(
        start_kernel,
        out_shape=[jax.ShapeDtypeStruct((tok, width + TAIL), BF)] * 2,
        in_specs=[pl.BlockSpec(memory_space=pltpu.SMEM)] + [pl.BlockSpec()] * 6,
        out_specs=vmem(2),
    )(
        core_arg,
        tokens,
        cotangent,
        node_routes.T,
        home_local,
        second_local.T,
        gate_weights.T,
    )
    chip = jnp.concatenate([raw_keep, across(raw_send)], axis=0)
    rows = jnp.concatenate(
        [chip, along_x(chip, 1), along_x(chip, -1), along_x(chip, 2)], axis=0
    )

    weights = rows[:, half : half + experts]
    count = rows.shape[0]
    groups = count // tok
    slots = groups * cap
    nearby = 4 * x_pos + (z_pos + jnp.arange(4, dtype=jnp.int32)) % 4
    in_node = (jnp.arange(experts, dtype=jnp.int32)[:, None] // 4 == nearby[None, :]).astype(BF)
    member = nn((weights != 0).astype(BF), in_node) > 0
    row = jnp.arange(count, dtype=jnp.int32)
    before = (row[:, None] // tok == row[None, :] // tok) & (row[:, None] > row[None, :])
    rank = nn(before.astype(BF), member.astype(BF)).astype(jnp.int32)
    group = row // tok
    place = ((group // 2 * 2 + (group + core) % 2) * cap)[:, None] + rank
    place = jnp.where(member, place, -1)
    select = (
        (place.T[:, None, :] == jnp.arange(slots, dtype=jnp.int32)[None, :, None])
        .astype(BF)
        .reshape(4 * slots, count)
    )
    parts = jnp.split(nn(select, rows).astype(BF), 4, axis=0)
    side = 2 * slots

    hid_width = gate_w.shape[2]
    gate_own, gate_oth, up_own, up_oth, down_own, down_oth = pl.pallas_call(
        weight_kernel,
        out_shape=[jax.ShapeDtypeStruct((half + TAIL, hid_width), BF)] * 4
        + [jax.ShapeDtypeStruct((hid_width, half), BF)] * 2,
        in_specs=[pl.BlockSpec(memory_space=pltpu.SMEM)] + [anywhere] * 4,
        out_specs=vmem(6),
        scratch_shapes=[pltpu.SemaphoreType.DMA((6,))],
    )(core_arg, gate_w[0], up_w[0], down_w[0], raw_send)

    mine = jnp.concatenate(exchange_z(parts, 1), axis=0)
    below, above = along_y(mine, 1), along_y(mine, -1)
    far = jnp.concatenate([along_y(below[:side], 1), along_y(above[side:], -1)], axis=0)
    near = jnp.concatenate([mine, below, above], axis=0)
    own = jnp.concatenate([near, far], axis=0)
    oth = jnp.concatenate([across(near), across(far)], axis=0)
    x_own, d_own = own[:, : half + TAIL], own[:, half + TAIL :]
    x_oth, d_oth = oth[:, : half + TAIL], oth[:, half + TAIL :]

    tail_lane = jnp.arange(TAIL, dtype=jnp.int32)[None, :]
    weight = jnp.sum(
        jnp.where(tail_lane == my_expert, x_own[:, half:].astype(F32), 0.0),
        axis=1,
        keepdims=True,
    )
    pre_gate = nn(x_own, gate_own) + nn(x_oth, gate_oth)
    pre_up = nn(x_own, up_own) + nn(x_oth, up_oth)
    activated, slope = silu_parts(pre_gate)
    hidden = (activated * pre_up).astype(BF)
    scaled = (weight * hidden.astype(F32)).astype(BF)
    hidden, scaled, for_gate, for_up = lax.optimization_barrier(
        (hidden, scaled, weight * (pre_up * slope), weight * activated)
    )
    hidden_grad = nt(d_own, down_own) + nt(d_oth, down_oth)
    gate_grad = (hidden_grad * for_gate).astype(BF)
    up_grad = (hidden_grad * for_up).astype(BF)
    send = (nt(gate_grad, gate_oth) + nt(up_grad, up_oth)).astype(BF)
    got = across(send)
    keep = nt(gate_grad, gate_own) + nt(up_grad, up_own)
    router = jnp.sum(hidden_grad * hidden.astype(F32), axis=1)
    router = jnp.where(weight[:, 0] != 0, router, 0.0)
    router = (router + across(router))[:, None]
    high = router.astype(BF).astype(F32)
    column = jnp.arange(half + TAIL, dtype=jnp.int32)[None, :]
    full = keep + got.astype(F32)
    full = jnp.where(column == half + my_expert, high, full)
    full = jnp.where(column == half + TAIL // 2 + my_expert, router - high, full).astype(BF)
    pieces = lax.optimization_barrier(tuple(jnp.split(full, 8, axis=0)))
    own_top, own_bottom, below_top, below_bottom, above_top, above_bottom = pieces[:6]
    far_top, far_bottom = pieces[6:]
    from_above = along_y(far_top, -1)
    from_below = along_y(far_bottom, 1)
    early_top, early_bottom = along_y(above_top, 1), along_y(below_bottom, -1)
    late_top = along_y(below_top + from_above, -1)
    late_bottom = along_y(above_bottom + from_below, 1)

    def add(*parts):
        return sum(p.astype(F32) for p in parts).astype(BF)

    top_rows = add(own_top, early_top, late_top)
    bottom_rows = add(own_bottom, early_bottom, late_bottom)
    back = [top_rows[:slots], top_rows[slots:], bottom_rows[:slots], bottom_rows[slots:]]
    back = jnp.concatenate(exchange_z(back, -1), axis=0)
    parts = jnp.split(tn(select, back).astype(BF), 4, axis=0)
    parts = [parts[0], along_x(parts[1], -1), along_x(parts[2], 1), along_x(parts[3], 2)]
    chip = sum(p.astype(F32) for p in parts)
    theirs = across(chip[tok:, :half].astype(BF))
    mine = chip[:tok]
    mine_cols = mine[:, :half].astype(BF)
    d_tokens = jnp.concatenate(
        [jnp.where(first, mine_cols, theirs), jnp.where(first, theirs, mine_cols)], axis=1
    )
    by_expert = mine[:, half : half + TAIL // 2] + mine[:, half + TAIL // 2 :]
    by_expert = jnp.concatenate([by_expert, jnp.zeros_like(by_expert)], axis=1)
    lane16 = jnp.arange(home_local.shape[1], dtype=jnp.int32)
    node_match = node_routes[:, :, None] == lane16[None, None, :]
    home = jnp.sum(jnp.where(node_match, home_local[0][None, None, :], 0), axis=2)
    other = (home + jnp.maximum(second_local, 1)) % 4
    ids = jnp.repeat(node_routes, 2, axis=1) * 4 + jnp.stack([home, other], axis=2).reshape(tok, top)
    onehot = ids[:, :, None] == jnp.arange(TAIL, dtype=jnp.int32)[None, None, :]
    d_gates = jnp.sum(jnp.where(onehot, by_expert[:, None, :], 0.0), axis=2).astype(BF)

    def whole(mine, theirs):
        return jnp.where(
            first,
            jnp.concatenate([mine, theirs], axis=1),
            jnp.concatenate([theirs, mine], axis=1),
        )

    x_all = whole(x_own[:, :half], x_oth[:, :half])
    d_all = whole(d_own, d_oth)
    return (
        d_tokens,
        d_gates,
        tn(x_all, gate_grad).astype(BF)[None],
        tn(x_all, up_grad).astype(BF)[None],
        tn(scaled, d_all).astype(BF)[None],
    )


def solution(mesh):
    rows = P(("node", "local"), None)
    blocks = P(("node", "local"), None, None)
    return jax.shard_map(
        per_device,
        mesh=mesh,
        in_specs=(rows,) * 6 + (blocks,) * 3,
        out_specs=(rows, rows, blocks, blocks, blocks),
        check_vma=False,
    )
```

```python
import jax
import jax.numpy as jnp
from jax import lax
from jax.experimental import pallas as pl
from jax.experimental.pallas import tpu as pltpu
from jax.sharding import PartitionSpec as P

BF = jnp.bfloat16
F32 = jnp.float32
TAIL = 128


def along_x(value, step):
    pairs = [(x * 4 + z, (x + step) % 4 * 4 + z) for x in range(4) for z in range(4)]
    return lax.ppermute(value, "node", pairs)


def along_z(value, step):
    pairs = [(x * 4 + z, x * 4 + (z + step) % 4) for x in range(4) for z in range(4)]
    return lax.ppermute(value, "node", pairs)


def along_y(value, step):
    pairs = [(y * 2 + c, (y + step) % 4 * 2 + c) for y in range(4) for c in range(2)]
    return lax.ppermute(value, "local", pairs)


def across(value):
    return lax.ppermute(value, "local", [(i, i ^ 1) for i in range(8)])


def dot(left, right, dims):
    return lax.dot_general(left, right, ((dims[0], dims[1]), ((), ())), preferred_element_type=F32)


def silu_parts(pre_gate):
    sigmoid = jax.nn.sigmoid(pre_gate)
    return (pre_gate * sigmoid, sigmoid * (1.0 + pre_gate * (1.0 - sigmoid)))


def exchange_z(parts, sign):
    return [parts[0]] + [along_z(parts[k], sign * k) for k in (1, 2, 3)]


def nn(left, right):
    return dot(left, right, ((1,), (0,)))


def nt(left, right):
    return dot(left, right, ((1,), (1,)))


def tn(left, right):
    return dot(left, right, ((0,), (0,)))


def vmem(count):
    return [pl.BlockSpec(memory_space=pltpu.VMEM)] * count


def start_kernel(core, tok, cot, routes, homes, second, weights, keep, send):
    rows, width = tok.shape
    half = width // 2
    nodes = homes.shape[1]
    first = core[0] == 0
    lane = lax.broadcasted_iota(jnp.int32, (TAIL, rows), 0)
    row_id = lax.broadcasted_iota(jnp.int32, (nodes, nodes), 0)
    col_id = lax.broadcasted_iota(jnp.int32, (nodes, nodes), 1)
    home_col = jnp.sum(jnp.where(row_id == col_id, homes[...], 0), axis=1, keepdims=True)
    node_id = lax.broadcasted_iota(jnp.int32, (nodes, rows), 0)
    tail = jnp.zeros((TAIL, rows), F32)
    for j in range(routes.shape[0]):
        node = routes[j : j + 1, :]
        home = jnp.sum(jnp.where(node_id == node, home_col, 0), axis=0, keepdims=True)
        other = lax.rem(home + jnp.maximum(second[j : j + 1, :], 1), 4)
        for k, pick in ((2 * j, home), (2 * j + 1, other)):
            weight = weights[k : k + 1, :].astype(F32)
            tail = tail + jnp.where(lane == node * 4 + pick, weight, 0.0)
    tail = tail.T.astype(BF)
    for out, is_left in ((keep, first), (send, jnp.logical_not(first))):
        out[:, :half] = jnp.where(is_left, tok[:, :half], tok[:, half:])
        out[:, half : half + TAIL] = tail
        out[:, half + TAIL :] = jnp.where(is_left, cot[:, :half], cot[:, half:])


def weight_kernel(core, gate, up, down, _, gate_own, gate_oth, up_own, up_oth, down_own, down_oth, sems):
    half = down_own.shape[1]
    copies = []
    for src, outs in ((gate, (gate_own, gate_oth)), (up, (up_own, up_oth))):
        for out, which in zip(outs, (core[0], 1 - core[0])):
            rows = pl.ds(pl.multiple_of(which * half, half), half)
            copies.append((src.at[rows, :], out.at[pl.ds(0, half), :]))
    for out, which in ((down_own, core[0]), (down_oth, 1 - core[0])):
        cols = pl.ds(pl.multiple_of(which * half, half), half)
        copies.append((down.at[:, cols], out))
    copies = [
        pltpu.make_async_copy(src, dst, sems.at[i]) for i, (src, dst) in enumerate(copies)
    ]
    for copy in copies:
        copy.start()
    for out in (gate_own, gate_oth, up_own, up_oth):
        out[half:, :] = jnp.zeros((out.shape[0] - half, out.shape[1]), BF)
    for copy in copies:
        copy.wait()


def stack_kernel(top, bottom, _, out):
    side = top.shape[0]
    out[:side, :] = top[...]
    out[side:, :] = bottom[...]


def per_device(
    tokens, cotangent, node_routes, home_local, second_local, gate_weights, gate_w, up_w, down_w
):
    tok, width = tokens.shape
    half = width // 2
    top = gate_weights.shape[1]
    cap = 5
    experts = lax.axis_size("node") * 4
    node = lax.axis_index("node")
    local = lax.axis_index("local")
    x_pos, z_pos = node // 4, node % 4
    core = local % 2
    first = core == 0
    my_expert = 4 * node + local // 2
    core_arg = core.astype(jnp.int32).reshape(1)
    anywhere = pl.BlockSpec(memory_space=pl.ANY)

    raw_keep, raw_send = pl.pallas_call(
        start_kernel,
        out_shape=[jax.ShapeDtypeStruct((tok, width + TAIL), BF)] * 2,
        in_specs=[pl.BlockSpec(memory_space=pltpu.SMEM)] + [pl.BlockSpec()] * 6,
        out_specs=vmem(2),
    )(
        core_arg,
        tokens,
        cotangent,
        node_routes.T,
        home_local,
        second_local.T,
        gate_weights.T,
    )
    chip = jnp.concatenate([raw_keep, across(raw_send)], axis=0)
    rows = jnp.concatenate(
        [chip, along_x(chip, 1), along_x(chip, -1), along_x(chip, 2)], axis=0
    )

    weights = rows[:, half : half + experts]
    count = rows.shape[0]
    groups = count // tok
    slots = groups * cap
    nearby = 4 * x_pos + (z_pos + jnp.arange(4, dtype=jnp.int32)) % 4
    in_node = (jnp.arange(experts, dtype=jnp.int32)[:, None] // 4 == nearby[None, :]).astype(BF)
    member = nn((weights != 0).astype(BF), in_node) > 0
    row = jnp.arange(count, dtype=jnp.int32)
    before = (row[:, None] // tok == row[None, :] // tok) & (row[:, None] > row[None, :])
    rank = nn(before.astype(BF), member.astype(BF)).astype(jnp.int32)
    group = row // tok
    place = ((group // 2 * 2 + (group + core) % 2) * cap)[:, None] + rank
    place = jnp.where(member, place, -1)
    select = (
        (place.T[:, None, :] == jnp.arange(slots, dtype=jnp.int32)[None, :, None])
        .astype(BF)
        .reshape(4 * slots, count)
    )
    parts = jnp.split(nn(select, rows).astype(BF), 4, axis=0)
    side = 2 * slots

    hid_width = gate_w.shape[2]
    gate_own, gate_oth, up_own, up_oth, down_own, down_oth = pl.pallas_call(
        weight_kernel,
        out_shape=[jax.ShapeDtypeStruct((half + TAIL, hid_width), BF)] * 4
        + [jax.ShapeDtypeStruct((hid_width, half), BF)] * 2,
        in_specs=[pl.BlockSpec(memory_space=pltpu.SMEM)]
        + [pl.BlockSpec(memory_space=pltpu.HBM)] * 3
        + [anywhere],
        out_specs=vmem(6),
        scratch_shapes=[pltpu.SemaphoreType.DMA((6,))],
    )(core_arg, gate_w[0], up_w[0], down_w[0], raw_send)

    mine = jnp.concatenate(exchange_z(parts, 1), axis=0)
    below, above = along_y(mine, 1), along_y(mine, -1)
    far_parts = along_y(below[:side], 1), along_y(above[side:], -1)
    near = [mine, below, above]
    tail_lane = jnp.arange(TAIL, dtype=jnp.int32)[None, :]

    def row_gradients(own, oth):
        x_own, d_own = own[:, : half + TAIL], own[:, half + TAIL :]
        x_oth, d_oth = oth[:, : half + TAIL], oth[:, half + TAIL :]
        weight = jnp.sum(
            jnp.where(tail_lane == my_expert, x_own[:, half:].astype(F32), 0.0),
            axis=1,
            keepdims=True,
        )
        pre_gate = nn(x_own, gate_own) + nn(x_oth, gate_oth)
        pre_up = nn(x_own, up_own) + nn(x_oth, up_oth)
        activated, slope = silu_parts(pre_gate)
        hidden = (activated * pre_up).astype(BF)
        scaled = (weight * hidden.astype(F32)).astype(BF)
        hidden, scaled, for_gate, for_up = lax.optimization_barrier(
            (hidden, scaled, weight * (pre_up * slope), weight * activated)
        )
        hidden_grad = nt(d_own, down_own) + nt(d_oth, down_oth)
        gate_grad = (hidden_grad * for_gate).astype(BF)
        up_grad = (hidden_grad * for_up).astype(BF)
        got = across((nt(gate_grad, gate_oth) + nt(up_grad, up_oth)).astype(BF)[:, :half])
        keep = nt(gate_grad, gate_own) + nt(up_grad, up_own)
        router = jnp.sum(hidden_grad * hidden.astype(F32), axis=1)
        router = jnp.where(weight[:, 0] != 0, router, 0.0)
        router = (router + across(router))[:, None]
        high = router.astype(BF).astype(F32)
        tail = jnp.where(tail_lane == my_expert, high, 0.0)
        tail = jnp.where(tail_lane == my_expert + TAIL // 2, router - high, tail).astype(BF)
        full = (keep[:, :half] + got.astype(F32)).astype(BF)
        full = jnp.concatenate([full, tail], axis=1)
        pieces = lax.optimization_barrier(tuple(jnp.split(full, own.shape[0] // side, axis=0)))
        return (own, oth, gate_grad, up_grad, scaled), pieces

    near_state, pieces = row_gradients(
        jnp.concatenate(near, axis=0), jnp.concatenate([across(p) for p in near], axis=0)
    )
    own_top, own_bottom, below_top, below_bottom, above_top, above_bottom = pieces
    far = pl.pallas_call(
        stack_kernel,
        out_shape=jax.ShapeDtypeStruct((2 * side, rows.shape[1]), BF),
        in_specs=vmem(3),
        out_specs=vmem(1)[0],
    )(*far_parts, near_state[2])
    far_state, (far_top, far_bottom) = row_gradients(far, across(far))
    from_above = along_y(far_top, -1)
    from_below = along_y(far_bottom, 1)
    early_top, early_bottom = along_y(above_top, 1), along_y(below_bottom, -1)
    late_top = along_y(below_top + from_above, -1)
    late_bottom = along_y(above_bottom + from_below, 1)

    def add(*parts):
        return sum(p.astype(F32) for p in parts).astype(BF)

    top_rows = add(own_top, early_top, late_top)
    bottom_rows = add(own_bottom, early_bottom, late_bottom)
    back = [top_rows[:slots], top_rows[slots:], bottom_rows[:slots], bottom_rows[slots:]]
    back = jnp.concatenate(exchange_z(back, -1), axis=0)
    parts = jnp.split(tn(select, back).astype(BF), 4, axis=0)
    parts = [parts[0], along_x(parts[1], -1), along_x(parts[2], 1), along_x(parts[3], 2)]
    chip = sum(p.astype(F32) for p in parts)
    theirs = across(chip[tok:, :half].astype(BF))
    mine = chip[:tok]
    mine_cols = mine[:, :half].astype(BF)
    d_tokens = jnp.concatenate(
        [jnp.where(first, mine_cols, theirs), jnp.where(first, theirs, mine_cols)], axis=1
    )
    by_expert = mine[:, half : half + TAIL // 2] + mine[:, half + TAIL // 2 :]
    by_expert = jnp.concatenate([by_expert, jnp.zeros_like(by_expert)], axis=1)
    lane16 = jnp.arange(home_local.shape[1], dtype=jnp.int32)
    node_match = node_routes[:, :, None] == lane16[None, None, :]
    home = jnp.sum(jnp.where(node_match, home_local[0][None, None, :], 0), axis=2)
    other = (home + jnp.maximum(second_local, 1)) % 4
    ids = jnp.repeat(node_routes, 2, axis=1) * 4 + jnp.stack([home, other], axis=2).reshape(tok, top)
    onehot = ids[:, :, None] == jnp.arange(TAIL, dtype=jnp.int32)[None, None, :]
    d_gates = jnp.sum(jnp.where(onehot, by_expert[:, None, :], 0.0), axis=2).astype(BF)

    own, oth, gate_grad, up_grad, scaled = [
        jnp.concatenate(both, axis=0)
        for both in zip(near_state, far_state)
    ]

    def whole(mine, theirs):
        return jnp.where(
            first,
            jnp.concatenate([mine, theirs], axis=1),
            jnp.concatenate([theirs, mine], axis=1),
        )

    x_all = whole(own[:, :half], oth[:, :half])
    d_all = whole(own[:, half + TAIL :], oth[:, half + TAIL :])
    return (
        d_tokens,
        d_gates,
        tn(x_all, gate_grad).astype(BF)[None],
        tn(x_all, up_grad).astype(BF)[None],
        tn(scaled, d_all).astype(BF)[None],
    )


def solution(mesh):
    rows = P(("node", "local"), None)
    blocks = P(("node", "local"), None, None)
    return jax.shard_map(
        per_device,
        mesh=mesh,
        in_specs=(rows,) * 6 + (blocks,) * 3,
        out_specs=(rows, rows, blocks, blocks, blocks),
        check_vma=False,
    )
```

```python
import jax
import jax.numpy as jnp
from jax import lax
from jax.experimental import pallas as pl
from jax.experimental.pallas import tpu as pltpu
from jax.sharding import PartitionSpec as P

BF = jnp.bfloat16
F32 = jnp.float32
TAIL = 128


def along_x(value, step):
    pairs = [(x * 4 + z, (x + step) % 4 * 4 + z) for x in range(4) for z in range(4)]
    return lax.ppermute(value, "node", pairs)


def along_z(value, step):
    pairs = [(x * 4 + z, x * 4 + (z + step) % 4) for x in range(4) for z in range(4)]
    return lax.ppermute(value, "node", pairs)


def along_y(value, step):
    pairs = [(y * 2 + c, (y + step) % 4 * 2 + c) for y in range(4) for c in range(2)]
    return lax.ppermute(value, "local", pairs)


def across(value):
    return lax.ppermute(value, "local", [(i, i ^ 1) for i in range(8)])


def dot(left, right, dims):
    return lax.dot_general(left, right, ((dims[0], dims[1]), ((), ())), preferred_element_type=F32)


def silu_parts(pre_gate):
    sigmoid = jax.nn.sigmoid(pre_gate)
    return (pre_gate * sigmoid, sigmoid * (1.0 + pre_gate * (1.0 - sigmoid)))


def exchange_z(parts, sign):
    return [parts[0]] + [along_z(parts[k], sign * k) for k in (1, 2, 3)]


def nn(left, right):
    return dot(left, right, ((1,), (0,)))


def nt(left, right):
    return dot(left, right, ((1,), (1,)))


def tn(left, right):
    return dot(left, right, ((0,), (0,)))


def limit(mebibytes):
    return pltpu.CompilerParams(vmem_limit_bytes=mebibytes * 1024 * 1024)


def vmem(count):
    return [pl.BlockSpec(memory_space=pltpu.VMEM)] * count


def start_kernel(core, tok, cot, routes, homes, second, weights, keep, send):
    rows, width = tok.shape
    half = width // 2
    nodes = homes.shape[1]
    first = core[0] == 0
    lane = lax.broadcasted_iota(jnp.int32, (TAIL, rows), 0)
    row_id = lax.broadcasted_iota(jnp.int32, (nodes, nodes), 0)
    col_id = lax.broadcasted_iota(jnp.int32, (nodes, nodes), 1)
    home_col = jnp.sum(jnp.where(row_id == col_id, homes[...], 0), axis=1, keepdims=True)
    node_id = lax.broadcasted_iota(jnp.int32, (nodes, rows), 0)
    tail = jnp.zeros((TAIL, rows), F32)
    for j in range(routes.shape[0]):
        node = routes[j : j + 1, :]
        home = jnp.sum(jnp.where(node_id == node, home_col, 0), axis=0, keepdims=True)
        other = lax.rem(home + jnp.maximum(second[j : j + 1, :], 1), 4)
        for k, pick in ((2 * j, home), (2 * j + 1, other)):
            weight = weights[k : k + 1, :].astype(F32)
            tail = tail + jnp.where(lane == node * 4 + pick, weight, 0.0)
    tail = tail.T.astype(BF)
    for out, is_left in ((keep, first), (send, jnp.logical_not(first))):
        out[:, :half] = jnp.where(is_left, tok[:, :half], tok[:, half:])
        out[:, half : half + TAIL] = tail
        out[:, half + TAIL :] = jnp.where(is_left, cot[:, :half], cot[:, half:])


def weight_kernel(core, gate, up, down, _, own, oth, down_own, down_oth, sems):
    half = down_own.shape[1]
    hid_width = gate.shape[1]
    copies = []
    for out, down_out, which in ((own, down_own, core[0]), (oth, down_oth, 1 - core[0])):
        place = pl.ds(pl.multiple_of(which * half, half), half)
        top = pl.ds(0, half)
        copies.append((gate.at[place, :], out.at[top, pl.ds(0, hid_width)]))
        copies.append((up.at[place, :], out.at[top, pl.ds(hid_width, hid_width)]))
        copies.append((down.at[:, place], down_out))
    copies = [
        pltpu.make_async_copy(src, dst, sems.at[i]) for i, (src, dst) in enumerate(copies)
    ]
    for copy in copies:
        copy.start()
    for out in (own, oth):
        out[half:, :] = jnp.zeros((out.shape[0] - half, out.shape[1]), BF)
    for copy in copies:
        copy.wait()


def stack_kernel(top, bottom, _, out):
    side = top.shape[0]
    out[:side, :] = top[...]
    out[side:, :] = bottom[...]


def per_device(
    tokens, cotangent, node_routes, home_local, second_local, gate_weights, gate_w, up_w, down_w
):
    tok, width = tokens.shape
    half = width // 2
    top = gate_weights.shape[1]
    cap = 5
    experts = lax.axis_size("node") * 4
    node = lax.axis_index("node")
    local = lax.axis_index("local")
    x_pos, z_pos = node // 4, node % 4
    core = local % 2
    first = core == 0
    my_expert = 4 * node + local // 2
    core_arg = core.astype(jnp.int32).reshape(1)
    anywhere = pl.BlockSpec(memory_space=pl.ANY)

    raw_keep, raw_send = pl.pallas_call(
        start_kernel,
        out_shape=[jax.ShapeDtypeStruct((tok, width + TAIL), BF)] * 2,
        in_specs=[pl.BlockSpec(memory_space=pltpu.SMEM)] + [pl.BlockSpec()] * 6,
        out_specs=vmem(2),
        compiler_params=limit(4),
    )(
        core_arg,
        tokens,
        cotangent,
        node_routes.T,
        home_local,
        second_local.T,
        gate_weights.T,
    )
    chip = jnp.concatenate([raw_keep, across(raw_send)], axis=0)
    rows = jnp.concatenate(
        [chip, along_x(chip, 1), along_x(chip, -1), along_x(chip, 2)], axis=0
    )

    weights = rows[:, half : half + experts]
    count = rows.shape[0]
    groups = count // tok
    slots = groups * cap
    nearby = 4 * x_pos + (z_pos + jnp.arange(4, dtype=jnp.int32)) % 4
    in_node = (jnp.arange(experts, dtype=jnp.int32)[:, None] // 4 == nearby[None, :]).astype(BF)
    member = nn((weights != 0).astype(BF), in_node) > 0
    row = jnp.arange(count, dtype=jnp.int32)
    before = (row[:, None] // tok == row[None, :] // tok) & (row[:, None] > row[None, :])
    rank = nn(before.astype(BF), member.astype(BF)).astype(jnp.int32)
    group = row // tok
    place = ((group // 2 * 2 + (group + core) % 2) * cap)[:, None] + rank
    place = jnp.where(member, place, -1)
    select = (
        (place.T[:, None, :] == jnp.arange(slots, dtype=jnp.int32)[None, :, None])
        .astype(BF)
        .reshape(4 * slots, count)
    )
    parts = jnp.split(nn(select, rows).astype(BF), 4, axis=0)
    side = 2 * slots

    hid_width = gate_w.shape[2]
    proj_own, proj_oth, down_own, down_oth = pl.pallas_call(
        weight_kernel,
        out_shape=[jax.ShapeDtypeStruct((half + TAIL, 2 * hid_width), BF)] * 2
        + [jax.ShapeDtypeStruct((hid_width, half), BF)] * 2,
        in_specs=[pl.BlockSpec(memory_space=pltpu.SMEM)]
        + [pl.BlockSpec(memory_space=pltpu.HBM)] * 3
        + [anywhere],
        out_specs=vmem(4),
        scratch_shapes=[pltpu.SemaphoreType.DMA((6,))],
        compiler_params=limit(14),
    )(core_arg, gate_w[0], up_w[0], down_w[0], raw_send)

    mine = jnp.concatenate(exchange_z(parts, 1), axis=0)
    below, above = along_y(mine, 1), along_y(mine, -1)
    far_parts = along_y(below[:side], 1), along_y(above[side:], -1)
    near = [mine, below, above]
    tail_lane = jnp.arange(TAIL, dtype=jnp.int32)[None, :]

    def row_gradients(own, oth):
        x_own, d_own = own[:, : half + TAIL], own[:, half + TAIL :]
        x_oth, d_oth = oth[:, : half + TAIL], oth[:, half + TAIL :]
        weight = jnp.sum(
            jnp.where(tail_lane == my_expert, x_own[:, half:].astype(F32), 0.0),
            axis=1,
            keepdims=True,
        )
        pre = nn(x_own, proj_own) + nn(x_oth, proj_oth)
        pre_gate, pre_up = pre[:, :hid_width], pre[:, hid_width:]
        activated, slope = silu_parts(pre_gate)
        hidden = (activated * pre_up).astype(BF)
        scaled = (weight * hidden.astype(F32)).astype(BF)
        hidden, scaled, for_gate, for_up = lax.optimization_barrier(
            (hidden, scaled, weight * (pre_up * slope), weight * activated)
        )
        hidden_grad = nt(d_own, down_own) + nt(d_oth, down_oth)
        grads = jnp.concatenate(
            [(hidden_grad * for_gate).astype(BF), (hidden_grad * for_up).astype(BF)], axis=1
        )
        got = across(nt(grads, proj_oth[:half]).astype(BF))
        keep = nt(grads, proj_own[:half])
        router = jnp.sum(hidden_grad * hidden.astype(F32), axis=1)
        router = jnp.where(weight[:, 0] != 0, router, 0.0)
        router = (router + across(router))[:, None]
        high = router.astype(BF).astype(F32)
        tail = jnp.where(tail_lane == my_expert, high, 0.0)
        tail = jnp.where(tail_lane == my_expert + TAIL // 2, router - high, tail).astype(BF)
        full = jnp.concatenate([(keep + got.astype(F32)).astype(BF), tail], axis=1)
        return (own, oth, grads, scaled), full

    near_state, near_full = row_gradients(
        jnp.concatenate(near, axis=0), jnp.concatenate([across(p) for p in near], axis=0)
    )
    far = pl.pallas_call(
        stack_kernel,
        out_shape=jax.ShapeDtypeStruct((2 * side, rows.shape[1]), BF),
        in_specs=vmem(3),
        out_specs=vmem(1)[0],
        compiler_params=limit(4),
    )(*far_parts, near_state[2])
    far_state, far_full = row_gradients(far, across(far))

    near_full, far_full = lax.optimization_barrier((near_full, far_full))
    own_top, own_bottom, below_top, below_bottom, above_top, above_bottom = jnp.split(
        near_full, 6, axis=0
    )
    from_above = along_y(jnp.concatenate([far_full[:side], below_bottom], axis=0), -1)
    from_below = along_y(jnp.concatenate([far_full[side:], above_top], axis=0), 1)
    early_top, early_bottom = from_below[side:], from_above[side:]
    late_top = along_y(below_top + from_above[:side], -1)
    late_bottom = along_y(above_bottom + from_below[:side], 1)

    def add(*parts):
        return sum(p.astype(F32) for p in parts).astype(BF)

    top_rows = add(own_top, early_top, late_top)
    bottom_rows = add(own_bottom, early_bottom, late_bottom)
    back = [top_rows[:slots], top_rows[slots:], bottom_rows[:slots], bottom_rows[slots:]]
    back = jnp.concatenate(exchange_z(back, -1), axis=0)
    parts = jnp.split(tn(select, back).astype(BF), 4, axis=0)
    parts = [parts[0], along_x(parts[1], -1), along_x(parts[2], 1), along_x(parts[3], 2)]
    chip = sum(p.astype(F32) for p in parts)
    theirs = across(chip[tok:, :half].astype(BF))
    mine = chip[:tok]
    mine_cols = mine[:, :half].astype(BF)
    d_tokens = jnp.concatenate(
        [jnp.where(first, mine_cols, theirs), jnp.where(first, theirs, mine_cols)], axis=1
    )
    by_expert = mine[:, half : half + TAIL // 2] + mine[:, half + TAIL // 2 :]
    by_expert = jnp.concatenate([by_expert, jnp.zeros_like(by_expert)], axis=1)
    lane16 = jnp.arange(home_local.shape[1], dtype=jnp.int32)
    node_match = node_routes[:, :, None] == lane16[None, None, :]
    home = jnp.sum(jnp.where(node_match, home_local[0][None, None, :], 0), axis=2)
    other = (home + jnp.maximum(second_local, 1)) % 4
    ids = jnp.repeat(node_routes, 2, axis=1) * 4 + jnp.stack([home, other], axis=2).reshape(tok, top)
    onehot = ids[:, :, None] == jnp.arange(TAIL, dtype=jnp.int32)[None, None, :]
    d_gates = jnp.sum(jnp.where(onehot, by_expert[:, None, :], 0.0), axis=2).astype(BF)

    own, oth, grads, scaled = [
        jnp.concatenate(both, axis=0)
        for both in zip(near_state, far_state)
    ]

    def whole(mine, theirs):
        return jnp.where(
            first,
            jnp.concatenate([mine, theirs], axis=1),
            jnp.concatenate([theirs, mine], axis=1),
        )

    x_all = whole(own[:, :half], oth[:, :half])
    d_all = whole(own[:, half + TAIL :], oth[:, half + TAIL :])
    return (
        d_tokens,
        d_gates,
        tn(x_all, grads[:, :hid_width]).astype(BF)[None],
        tn(x_all, grads[:, hid_width:]).astype(BF)[None],
        tn(scaled, d_all).astype(BF)[None],
    )


def solution(mesh):
    rows = P(("node", "local"), None)
    blocks = P(("node", "local"), None, None)
    return jax.shard_map(
        per_device,
        mesh=mesh,
        in_specs=(rows,) * 6 + (blocks,) * 3,
        out_specs=(rows, rows, blocks, blocks, blocks),
        check_vma=False,
    )
```

```python
import functools

import jax
import jax.numpy as jnp
from jax import lax
from jax.experimental import pallas as pl
from jax.experimental.pallas import tpu as pltpu
from jax.sharding import PartitionSpec as P

BF = jnp.bfloat16
F32 = jnp.float32
TAIL = 128


def along_x(value, step):
    pairs = [(x * 4 + z, (x + step) % 4 * 4 + z) for x in range(4) for z in range(4)]
    return lax.ppermute(value, "node", pairs)


def along_z(value, step):
    pairs = [(x * 4 + z, x * 4 + (z + step) % 4) for x in range(4) for z in range(4)]
    return lax.ppermute(value, "node", pairs)


def along_y(value, step):
    pairs = [(y * 2 + c, (y + step) % 4 * 2 + c) for y in range(4) for c in range(2)]
    return lax.ppermute(value, "local", pairs)


def across(value):
    return lax.ppermute(value, "local", [(i, i ^ 1) for i in range(8)])


def dot(left, right, dims):
    return lax.dot_general(left, right, ((dims[0], dims[1]), ((), ())), preferred_element_type=F32)


def silu_parts(pre_gate):
    sigmoid = jax.nn.sigmoid(pre_gate)
    return (pre_gate * sigmoid, sigmoid * (1.0 + pre_gate * (1.0 - sigmoid)))


def exchange_z(parts, sign):
    return [parts[0]] + [along_z(parts[k], sign * k) for k in (1, 2, 3)]


def nn(left, right):
    return dot(left, right, ((1,), (0,)))


def nt(left, right):
    return dot(left, right, ((1,), (1,)))


def tn(left, right):
    return dot(left, right, ((0,), (0,)))


def limit(mebibytes):
    return pltpu.CompilerParams(vmem_limit_bytes=mebibytes * 1024 * 1024)


def vmem(count):
    return [pl.BlockSpec(memory_space=pltpu.VMEM)] * count


def start_kernel(core, tok, cot, routes, homes, second, weights, keep, send):
    rows, width = tok.shape
    half = width // 2
    nodes = homes.shape[1]
    first = core[0] == 0
    lane = lax.broadcasted_iota(jnp.int32, (TAIL, rows), 0)
    row_id = lax.broadcasted_iota(jnp.int32, (nodes, nodes), 0)
    col_id = lax.broadcasted_iota(jnp.int32, (nodes, nodes), 1)
    home_col = jnp.sum(jnp.where(row_id == col_id, homes[...], 0), axis=1, keepdims=True)
    node_id = lax.broadcasted_iota(jnp.int32, (nodes, rows), 0)
    tail = jnp.zeros((TAIL, rows), F32)
    for j in range(routes.shape[0]):
        node = routes[j : j + 1, :]
        home = jnp.sum(jnp.where(node_id == node, home_col, 0), axis=0, keepdims=True)
        other = lax.rem(home + jnp.maximum(second[j : j + 1, :], 1), 4)
        for k, pick in ((2 * j, home), (2 * j + 1, other)):
            weight = weights[k : k + 1, :].astype(F32)
            tail = tail + jnp.where(lane == node * 4 + pick, weight, 0.0)
    tail = tail.T.astype(BF)
    for out, is_left in ((keep, first), (send, jnp.logical_not(first))):
        out[:, :half] = jnp.where(is_left, tok[:, :half], tok[:, half:])
        out[:, half : half + TAIL] = tail
        out[:, half + TAIL :] = jnp.where(is_left, cot[:, :half], cot[:, half:])


def weight_kernel(core, gate, up, down, _, own, oth, down_own, down_oth, sems):
    half = down_own.shape[1]
    hid_width = gate.shape[1]
    copies = []
    for out, down_out, which in ((own, down_own, core[0]), (oth, down_oth, 1 - core[0])):
        place = pl.ds(pl.multiple_of(which * half, half), half)
        top = pl.ds(0, half)
        copies.append((gate.at[place, :], out.at[top, pl.ds(0, hid_width)]))
        copies.append((up.at[place, :], out.at[top, pl.ds(hid_width, hid_width)]))
        copies.append((down.at[:, place], down_out))
    copies = [
        pltpu.make_async_copy(src, dst, sems.at[i]) for i, (src, dst) in enumerate(copies)
    ]
    for copy in copies:
        copy.start()
    for out in (own, oth):
        out[half:, :] = jnp.zeros((out.shape[0] - half, out.shape[1]), BF)
    for copy in copies:
        copy.wait()


def stack_kernel(count, *refs):
    start = 0
    for ref in refs[:count]:
        refs[-1][pl.ds(start, ref.shape[0]), :] = ref[...]
        start += ref.shape[0]


def stack(parts, *done):
    shape = (sum(part.shape[0] for part in parts), parts[0].shape[1])
    return pl.pallas_call(
        functools.partial(stack_kernel, len(parts)),
        out_shape=jax.ShapeDtypeStruct(shape, BF),
        in_specs=vmem(len(parts) + len(done)),
        out_specs=vmem(1)[0],
        compiler_params=limit(6),
    )(*parts, *done)


def per_device(
    tokens, cotangent, node_routes, home_local, second_local, gate_weights, gate_w, up_w, down_w
):
    tok, width = tokens.shape
    half = width // 2
    top = gate_weights.shape[1]
    cap = 5
    experts = lax.axis_size("node") * 4
    node = lax.axis_index("node")
    local = lax.axis_index("local")
    x_pos, z_pos = node // 4, node % 4
    core = local % 2
    first = core == 0
    my_expert = 4 * node + local // 2
    core_arg = core.astype(jnp.int32).reshape(1)
    anywhere = pl.BlockSpec(memory_space=pl.ANY)

    raw_keep, raw_send = pl.pallas_call(
        start_kernel,
        out_shape=[jax.ShapeDtypeStruct((tok, width + TAIL), BF)] * 2,
        in_specs=[pl.BlockSpec(memory_space=pltpu.SMEM)] + [pl.BlockSpec()] * 6,
        out_specs=vmem(2),
    )(
        core_arg,
        tokens,
        cotangent,
        node_routes.T,
        home_local,
        second_local.T,
        gate_weights.T,
    )
    chip = jnp.concatenate([raw_keep, across(raw_send)], axis=0)
    rows = jnp.concatenate(
        [chip, along_x(chip, 1), along_x(chip, -1), along_x(chip, 2)], axis=0
    )

    weights = rows[:, half : half + experts]
    count = rows.shape[0]
    groups = count // tok
    slots = groups * cap
    nearby = 4 * x_pos + (z_pos + jnp.arange(4, dtype=jnp.int32)) % 4
    in_node = (jnp.arange(experts, dtype=jnp.int32)[:, None] // 4 == nearby[None, :]).astype(BF)
    member = nn((weights != 0).astype(BF), in_node) > 0
    row = jnp.arange(count, dtype=jnp.int32)
    before = (row[:, None] // tok == row[None, :] // tok) & (row[:, None] > row[None, :])
    rank = nn(before.astype(BF), member.astype(BF)).astype(jnp.int32)
    group = row // tok
    place = ((group // 2 * 2 + (group + core) % 2) * cap)[:, None] + rank
    place = jnp.where(member, place, -1)
    select = (
        (place.T[:, None, :] == jnp.arange(slots, dtype=jnp.int32)[None, :, None])
        .astype(BF)
        .reshape(4 * slots, count)
    )
    parts = jnp.split(nn(select, rows).astype(BF), 4, axis=0)
    side = 2 * slots

    hid_width = gate_w.shape[2]
    proj_own, proj_oth, down_own, down_oth = pl.pallas_call(
        weight_kernel,
        out_shape=[jax.ShapeDtypeStruct((half + TAIL, 2 * hid_width), BF)] * 2
        + [jax.ShapeDtypeStruct((hid_width, half), BF)] * 2,
        in_specs=[pl.BlockSpec(memory_space=pltpu.SMEM)]
        + [pl.BlockSpec(memory_space=pltpu.HBM)] * 3
        + [anywhere],
        out_specs=vmem(4),
        scratch_shapes=[pltpu.SemaphoreType.DMA((6,))],
        compiler_params=limit(14),
    )(core_arg, gate_w[0], up_w[0], down_w[0], raw_send)

    parts = exchange_z(parts, 1)
    first_below, first_above = along_y(parts[0], 1), along_y(parts[0], -1)
    rest = stack(parts[1:], first_below, first_above)
    mine = jnp.concatenate([parts[0], rest], axis=0)
    below = jnp.concatenate([first_below, along_y(rest, 1)], axis=0)
    above = jnp.concatenate([first_above, along_y(rest, -1)], axis=0)
    far_parts = along_y(below[:side], 1), along_y(above[side:], -1)
    near = [mine, below, above]
    tail_lane = jnp.arange(TAIL, dtype=jnp.int32)[None, :]

    def row_gradients(own, oth):
        x_own, d_own = own[:, : half + TAIL], own[:, half + TAIL :]
        x_oth, d_oth = oth[:, : half + TAIL], oth[:, half + TAIL :]
        weight = jnp.sum(
            jnp.where(tail_lane == my_expert, x_own[:, half:].astype(F32), 0.0),
            axis=1,
            keepdims=True,
        )
        pre = nn(x_own, proj_own) + nn(x_oth, proj_oth)
        pre_gate, pre_up = pre[:, :hid_width], pre[:, hid_width:]
        activated, slope = silu_parts(pre_gate)
        hidden = (activated * pre_up).astype(BF)
        scaled = (weight * hidden.astype(F32)).astype(BF)
        hidden, scaled, for_gate, for_up = lax.optimization_barrier(
            (hidden, scaled, weight * (pre_up * slope), weight * activated)
        )
        hidden_grad = nt(d_own, down_own) + nt(d_oth, down_oth)
        grads = jnp.concatenate(
            [(hidden_grad * for_gate).astype(BF), (hidden_grad * for_up).astype(BF)], axis=1
        )
        got = across(nt(grads, proj_oth[:half]).astype(BF))
        keep = nt(grads, proj_own[:half])
        router = jnp.sum(hidden_grad * hidden.astype(F32), axis=1)
        router = jnp.where(weight[:, 0] != 0, router, 0.0)
        router = (router + across(router))[:, None]
        high = router.astype(BF).astype(F32)
        tail = jnp.where(tail_lane == my_expert, high, 0.0)
        tail = jnp.where(tail_lane == my_expert + TAIL // 2, router - high, tail).astype(BF)
        full = jnp.concatenate([(keep + got.astype(F32)).astype(BF), tail], axis=1)
        return (own, oth, grads, scaled), full

    near_state, near_full = row_gradients(
        jnp.concatenate(near, axis=0), jnp.concatenate([across(p) for p in near], axis=0)
    )
    far = stack(far_parts, near_state[2])
    far_state, far_full = row_gradients(far, across(far))

    near_full, far_full = lax.optimization_barrier((near_full, far_full))
    own_rows, below_rows, above_rows = jnp.split(near_full, 3, axis=0)
    back_parts = [
        own_rows,
        along_y(below_rows, -1),
        along_y(above_rows, 1),
        along_y(far_full, 2),
    ]

    def add(*parts):
        return sum(p.astype(F32) for p in parts).astype(BF)

    back = jnp.split(add(*back_parts), 4, axis=0)
    back = jnp.concatenate(exchange_z(back, -1), axis=0)
    parts = jnp.split(tn(select, back).astype(BF), 4, axis=0)
    parts = [parts[0], along_x(parts[1], -1), along_x(parts[2], 1), along_x(parts[3], 2)]
    chip = sum(p.astype(F32) for p in parts)
    theirs = across(chip[tok:, :half].astype(BF))
    mine = chip[:tok]
    mine_cols = mine[:, :half].astype(BF)
    d_tokens = jnp.concatenate(
        [jnp.where(first, mine_cols, theirs), jnp.where(first, theirs, mine_cols)], axis=1
    )
    by_expert = mine[:, half : half + TAIL // 2] + mine[:, half + TAIL // 2 :]
    by_expert = jnp.concatenate([by_expert, jnp.zeros_like(by_expert)], axis=1)
    lane16 = jnp.arange(home_local.shape[1], dtype=jnp.int32)
    node_match = node_routes[:, :, None] == lane16[None, None, :]
    home = jnp.sum(jnp.where(node_match, home_local[0][None, None, :], 0), axis=2)
    other = (home + jnp.maximum(second_local, 1)) % 4
    ids = jnp.repeat(node_routes, 2, axis=1) * 4 + jnp.stack([home, other], axis=2).reshape(tok, top)
    onehot = ids[:, :, None] == jnp.arange(TAIL, dtype=jnp.int32)[None, None, :]
    d_gates = jnp.sum(jnp.where(onehot, by_expert[:, None, :], 0.0), axis=2).astype(BF)

    own, oth, grads, scaled = [
        jnp.concatenate(both, axis=0)
        for both in zip(near_state, far_state)
    ]

    def whole(mine, theirs):
        return jnp.where(
            first,
            jnp.concatenate([mine, theirs], axis=1),
            jnp.concatenate([theirs, mine], axis=1),
        )

    x_all = whole(own[:, :half], oth[:, :half])
    d_all = whole(own[:, half + TAIL :], oth[:, half + TAIL :])
    return (
        d_tokens,
        d_gates,
        tn(x_all, grads[:, :hid_width]).astype(BF)[None],
        tn(x_all, grads[:, hid_width:]).astype(BF)[None],
        tn(scaled, d_all).astype(BF)[None],
    )


def solution(mesh):
    rows = P(("node", "local"), None)
    blocks = P(("node", "local"), None, None)
    return jax.shard_map(
        per_device,
        mesh=mesh,
        in_specs=(rows,) * 6 + (blocks,) * 3,
        out_specs=(rows, rows, blocks, blocks, blocks),
        check_vma=False,
    )
```

```python
import functools

import jax
import jax.numpy as jnp
from jax import lax
from jax.experimental import pallas as pl
from jax.experimental.pallas import tpu as pltpu
from jax.sharding import PartitionSpec as P

BF = jnp.bfloat16
F32 = jnp.float32
TAIL = 128


def along_x(value, step):
    pairs = [(x * 4 + z, (x + step) % 4 * 4 + z) for x in range(4) for z in range(4)]
    return lax.ppermute(value, "node", pairs)


def along_z(value, step):
    pairs = [(x * 4 + z, x * 4 + (z + step) % 4) for x in range(4) for z in range(4)]
    return lax.ppermute(value, "node", pairs)


def along_y(value, step):
    pairs = [(y * 2 + c, (y + step) % 4 * 2 + c) for y in range(4) for c in range(2)]
    return lax.ppermute(value, "local", pairs)


def across(value):
    return lax.ppermute(value, "local", [(i, i ^ 1) for i in range(8)])


def dot(left, right, dims):
    return lax.dot_general(left, right, ((dims[0], dims[1]), ((), ())), preferred_element_type=F32)


def silu_parts(pre_gate):
    sigmoid = jax.nn.sigmoid(pre_gate)
    return (pre_gate * sigmoid, sigmoid * (1.0 + pre_gate * (1.0 - sigmoid)))


def exchange_z(parts, sign):
    return [parts[0]] + [along_z(parts[k], sign * k) for k in (1, 2, 3)]


def nn(left, right):
    return dot(left, right, ((1,), (0,)))


def nt(left, right):
    return dot(left, right, ((1,), (1,)))


def tn(left, right):
    return dot(left, right, ((0,), (0,)))


def limit(mebibytes):
    return pltpu.CompilerParams(vmem_limit_bytes=mebibytes * 1024 * 1024)


def vmem(count):
    return [pl.BlockSpec(memory_space=pltpu.VMEM)] * count


def start_kernel(core, tok, cot, routes, homes, second, weights, keep, send):
    rows, width = tok.shape
    half = width // 2
    nodes = homes.shape[1]
    first = core[0] == 0
    lane = lax.broadcasted_iota(jnp.int32, (TAIL, rows), 0)
    row_id = lax.broadcasted_iota(jnp.int32, (nodes, nodes), 0)
    col_id = lax.broadcasted_iota(jnp.int32, (nodes, nodes), 1)
    home_col = jnp.sum(jnp.where(row_id == col_id, homes[...], 0), axis=1, keepdims=True)
    node_id = lax.broadcasted_iota(jnp.int32, (nodes, rows), 0)
    tail = jnp.zeros((TAIL, rows), F32)
    for j in range(routes.shape[0]):
        node = routes[j : j + 1, :]
        home = jnp.sum(jnp.where(node_id == node, home_col, 0), axis=0, keepdims=True)
        other = lax.rem(home + jnp.maximum(second[j : j + 1, :], 1), 4)
        for k, pick in ((2 * j, home), (2 * j + 1, other)):
            weight = weights[k : k + 1, :].astype(F32)
            tail = tail + jnp.where(lane == node * 4 + pick, weight, 0.0)
    tail = tail.T.astype(BF)
    for out, is_left in ((keep, first), (send, jnp.logical_not(first))):
        out[:, :half] = jnp.where(is_left, tok[:, :half], tok[:, half:])
        out[:, half : half + TAIL] = tail
        out[:, half + TAIL :] = jnp.where(is_left, cot[:, :half], cot[:, half:])


def weight_kernel(core, gate, up, down, _, own, oth, down_own, down_oth, sems):
    half = down_own.shape[1]
    hid_width = gate.shape[1]
    copies = []
    for out, down_out, which in ((own, down_own, core[0]), (oth, down_oth, 1 - core[0])):
        place = pl.ds(pl.multiple_of(which * half, half), half)
        top = pl.ds(0, half)
        copies.append((gate.at[place, :], out.at[top, pl.ds(0, hid_width)]))
        copies.append((up.at[place, :], out.at[top, pl.ds(hid_width, hid_width)]))
        copies.append((down.at[:, place], down_out))
    copies = [
        pltpu.make_async_copy(src, dst, sems.at[i]) for i, (src, dst) in enumerate(copies)
    ]
    for copy in copies:
        copy.start()
    for out in (own, oth):
        out[half:, :] = jnp.zeros((out.shape[0] - half, out.shape[1]), BF)
    for copy in copies:
        copy.wait()


def stack_kernel(count, *refs):
    start = 0
    for ref in refs[:count]:
        refs[-1][pl.ds(start, ref.shape[0]), :] = ref[...]
        start += ref.shape[0]


def stack(parts, *done):
    shape = (sum(part.shape[0] for part in parts), parts[0].shape[1])
    return pl.pallas_call(
        functools.partial(stack_kernel, len(parts)),
        out_shape=jax.ShapeDtypeStruct(shape, BF),
        in_specs=vmem(len(parts) + len(done)),
        out_specs=vmem(1)[0],
        compiler_params=limit(6),
    )(*parts, *done)


def split_kernel(rows, _, __, top, bottom):
    side = top.shape[0]
    top[...] = rows[:side, :]
    bottom[...] = rows[side:, :]


def per_device(
    tokens, cotangent, node_routes, home_local, second_local, gate_weights, gate_w, up_w, down_w
):
    tok, width = tokens.shape
    half = width // 2
    top = gate_weights.shape[1]
    cap = 5
    experts = lax.axis_size("node") * 4
    node = lax.axis_index("node")
    local = lax.axis_index("local")
    x_pos, z_pos = node // 4, node % 4
    core = local % 2
    first = core == 0
    my_expert = 4 * node + local // 2
    core_arg = core.astype(jnp.int32).reshape(1)
    anywhere = pl.BlockSpec(memory_space=pl.ANY)

    raw_keep, raw_send = pl.pallas_call(
        start_kernel,
        out_shape=[jax.ShapeDtypeStruct((tok, width + TAIL), BF)] * 2,
        in_specs=[pl.BlockSpec(memory_space=pltpu.SMEM)] + [pl.BlockSpec()] * 6,
        out_specs=vmem(2),
    )(
        core_arg,
        tokens,
        cotangent,
        node_routes.T,
        home_local,
        second_local.T,
        gate_weights.T,
    )
    chip = jnp.concatenate([raw_keep, across(raw_send)], axis=0)
    rows = jnp.concatenate(
        [chip, along_x(chip, 1), along_x(chip, -1), along_x(chip, 2)], axis=0
    )

    weights = rows[:, half : half + experts]
    count = rows.shape[0]
    groups = count // tok
    slots = groups * cap
    nearby = 4 * x_pos + (z_pos + jnp.arange(4, dtype=jnp.int32)) % 4
    in_node = (jnp.arange(experts, dtype=jnp.int32)[:, None] // 4 == nearby[None, :]).astype(BF)
    member = nn((weights != 0).astype(BF), in_node) > 0
    row = jnp.arange(count, dtype=jnp.int32)
    before = (row[:, None] // tok == row[None, :] // tok) & (row[:, None] > row[None, :])
    rank = nn(before.astype(BF), member.astype(BF)).astype(jnp.int32)
    group = row // tok
    place = ((group // 2 * 2 + (group + core) % 2) * cap)[:, None] + rank
    place = jnp.where(member, place, -1)
    select = (
        (place.T[:, None, :] == jnp.arange(slots, dtype=jnp.int32)[None, :, None])
        .astype(BF)
        .reshape(4 * slots, count)
    )
    parts = jnp.split(nn(select, rows).astype(BF), 4, axis=0)
    side = 2 * slots

    hid_width = gate_w.shape[2]
    proj_own, proj_oth, down_own, down_oth = pl.pallas_call(
        weight_kernel,
        out_shape=[jax.ShapeDtypeStruct((half + TAIL, 2 * hid_width), BF)] * 2
        + [jax.ShapeDtypeStruct((hid_width, half), BF)] * 2,
        in_specs=[pl.BlockSpec(memory_space=pltpu.SMEM)]
        + [pl.BlockSpec(memory_space=pltpu.HBM)] * 3
        + [anywhere],
        out_specs=vmem(4),
        scratch_shapes=[pltpu.SemaphoreType.DMA((6,))],
        compiler_params=limit(14),
    )(core_arg, gate_w[0], up_w[0], down_w[0], raw_send)

    parts = exchange_z(parts, 1)
    first_below, first_above = along_y(parts[0], 1), along_y(parts[0], -1)
    rest = stack(parts[1:], first_below, first_above)
    mine = jnp.concatenate([parts[0], rest], axis=0)
    below = jnp.concatenate([first_below, along_y(rest, 1)], axis=0)
    above = jnp.concatenate([first_above, along_y(rest, -1)], axis=0)
    far_parts = along_y(below[:side], 1), along_y(above[side:], -1)
    near = [mine, below, above]
    tail_lane = jnp.arange(TAIL, dtype=jnp.int32)[None, :]

    def row_gradients(own, oth, *done):
        x_own, d_own = own[:, : half + TAIL], own[:, half + TAIL :]
        x_oth, d_oth = oth[:, : half + TAIL], oth[:, half + TAIL :]
        weight = jnp.sum(
            jnp.where(tail_lane == my_expert, x_own[:, half:].astype(F32), 0.0),
            axis=1,
            keepdims=True,
        )
        pre = nn(x_own, proj_own) + nn(x_oth, proj_oth)
        pre_gate, pre_up = pre[:, :hid_width], pre[:, hid_width:]
        activated, slope = silu_parts(pre_gate)
        hidden = (activated * pre_up).astype(BF)
        scaled = (weight * hidden.astype(F32)).astype(BF)
        hidden, scaled, for_gate, for_up = lax.optimization_barrier(
            (hidden, scaled, weight * (pre_up * slope), weight * activated)
        )
        hidden_grad = nt(d_own, down_own) + nt(d_oth, down_oth)
        grads = jnp.concatenate(
            [(hidden_grad * for_gate).astype(BF), (hidden_grad * for_up).astype(BF)], axis=1
        )
        if done:
            grads = stack([grads], *done)
        got = across(nt(grads, proj_oth[:half]).astype(BF))
        keep = nt(grads, proj_own[:half])
        router = jnp.sum(hidden_grad * hidden.astype(F32), axis=1)
        router = jnp.where(weight[:, 0] != 0, router, 0.0)
        router = (router + across(router))[:, None]
        high = router.astype(BF).astype(F32)
        tail = jnp.where(tail_lane == my_expert, high, 0.0)
        tail = jnp.where(tail_lane == my_expert + TAIL // 2, router - high, tail).astype(BF)
        full = jnp.concatenate([(keep + got.astype(F32)).astype(BF), tail], axis=1)
        return (own, oth, grads, scaled), full

    near_state, near_full = row_gradients(
        jnp.concatenate(near, axis=0), jnp.concatenate([across(p) for p in near], axis=0)
    )
    far = stack(far_parts, near_state[2])
    far_state, far_full = row_gradients(far, across(far), near_full)

    own_top, own_bottom, below_top, below_bottom, above_top, above_bottom = jnp.split(
        near_full, 6, axis=0
    )
    early_top, early_bottom = along_y(above_top, 1), along_y(below_bottom, -1)
    far_top, far_bottom = pl.pallas_call(
        split_kernel,
        out_shape=[jax.ShapeDtypeStruct((side, half + TAIL), BF)] * 2,
        in_specs=vmem(3),
        out_specs=vmem(2),
        compiler_params=limit(4),
    )(far_full, early_top, early_bottom)
    from_above, from_below = along_y(far_top, -1), along_y(far_bottom, 1)
    late_top = along_y(below_top + from_above, -1)
    late_bottom = along_y(above_bottom + from_below, 1)

    def add(*parts):
        return sum(p.astype(F32) for p in parts).astype(BF)

    top_rows = add(own_top, early_top, late_top)
    bottom_rows = add(own_bottom, early_bottom, late_bottom)
    back = [top_rows[:slots], top_rows[slots:], bottom_rows[:slots], bottom_rows[slots:]]
    back = jnp.concatenate(exchange_z(back, -1), axis=0)
    parts = jnp.split(tn(select, back).astype(BF), 4, axis=0)
    parts = [parts[0], along_x(parts[1], -1), along_x(parts[2], 1), along_x(parts[3], 2)]
    chip = sum(p.astype(F32) for p in parts)
    theirs = across(chip[tok:, :half].astype(BF))
    mine = chip[:tok]
    mine_cols = mine[:, :half].astype(BF)
    d_tokens = jnp.concatenate(
        [jnp.where(first, mine_cols, theirs), jnp.where(first, theirs, mine_cols)], axis=1
    )
    by_expert = mine[:, half : half + TAIL // 2] + mine[:, half + TAIL // 2 :]
    by_expert = jnp.concatenate([by_expert, jnp.zeros_like(by_expert)], axis=1)
    lane16 = jnp.arange(home_local.shape[1], dtype=jnp.int32)
    node_match = node_routes[:, :, None] == lane16[None, None, :]
    home = jnp.sum(jnp.where(node_match, home_local[0][None, None, :], 0), axis=2)
    other = (home + jnp.maximum(second_local, 1)) % 4
    ids = jnp.repeat(node_routes, 2, axis=1) * 4 + jnp.stack([home, other], axis=2).reshape(tok, top)
    onehot = ids[:, :, None] == jnp.arange(TAIL, dtype=jnp.int32)[None, None, :]
    d_gates = jnp.sum(jnp.where(onehot, by_expert[:, None, :], 0.0), axis=2).astype(BF)

    own, oth, grads, scaled = [
        jnp.concatenate(both, axis=0)
        for both in zip(near_state, far_state)
    ]

    def whole(mine, theirs):
        return jnp.where(
            first,
            jnp.concatenate([mine, theirs], axis=1),
            jnp.concatenate([theirs, mine], axis=1),
        )

    x_all = whole(own[:, :half], oth[:, :half])
    d_all = whole(own[:, half + TAIL :], oth[:, half + TAIL :])
    return (
        d_tokens,
        d_gates,
        tn(x_all, grads[:, :hid_width]).astype(BF)[None],
        tn(x_all, grads[:, hid_width:]).astype(BF)[None],
        tn(scaled, d_all).astype(BF)[None],
    )


def solution(mesh):
    rows = P(("node", "local"), None)
    blocks = P(("node", "local"), None, None)
    return jax.shard_map(
        per_device,
        mesh=mesh,
        in_specs=(rows,) * 6 + (blocks,) * 3,
        out_specs=(rows, rows, blocks, blocks, blocks),
        check_vma=False,
    )
```

```python
import functools

import jax
import jax.numpy as jnp
from jax import lax
from jax.experimental import pallas as pl
from jax.experimental.pallas import tpu as pltpu
from jax.sharding import PartitionSpec as P

BF = jnp.bfloat16
F32 = jnp.float32
TAIL = 128


def along_x(value, step):
    pairs = [(x * 4 + z, (x + step) % 4 * 4 + z) for x in range(4) for z in range(4)]
    return lax.ppermute(value, "node", pairs)


def along_z(value, step):
    pairs = [(x * 4 + z, x * 4 + (z + step) % 4) for x in range(4) for z in range(4)]
    return lax.ppermute(value, "node", pairs)


def along_y(value, step):
    pairs = [(y * 2 + c, (y + step) % 4 * 2 + c) for y in range(4) for c in range(2)]
    return lax.ppermute(value, "local", pairs)


def across(value):
    return lax.ppermute(value, "local", [(i, i ^ 1) for i in range(8)])


def dot(left, right, dims):
    return lax.dot_general(left, right, ((dims[0], dims[1]), ((), ())), preferred_element_type=F32)


def silu_parts(pre_gate):
    sigmoid = jax.nn.sigmoid(pre_gate)
    return (pre_gate * sigmoid, sigmoid * (1.0 + pre_gate * (1.0 - sigmoid)))


def exchange_z(parts, sign):
    return [parts[0]] + [along_z(parts[k], sign * k) for k in (1, 2, 3)]


def nn(left, right):
    return dot(left, right, ((1,), (0,)))


def nt(left, right):
    return dot(left, right, ((1,), (1,)))


def tn(left, right):
    return dot(left, right, ((0,), (0,)))


def limit(mebibytes):
    return pltpu.CompilerParams(vmem_limit_bytes=mebibytes * 1024 * 1024)


def vmem(count):
    return [pl.BlockSpec(memory_space=pltpu.VMEM)] * count


def start_kernel(core, tok, cot, routes, homes, second, weights, keep, send):
    rows, width = tok.shape
    half = width // 2
    nodes = homes.shape[1]
    first = core[0] == 0
    lane = lax.broadcasted_iota(jnp.int32, (TAIL, rows), 0)
    row_id = lax.broadcasted_iota(jnp.int32, (nodes, nodes), 0)
    col_id = lax.broadcasted_iota(jnp.int32, (nodes, nodes), 1)
    home_col = jnp.sum(jnp.where(row_id == col_id, homes[...], 0), axis=1, keepdims=True)
    node_id = lax.broadcasted_iota(jnp.int32, (nodes, rows), 0)
    tail = jnp.zeros((TAIL, rows), F32)
    for j in range(routes.shape[0]):
        node = routes[j : j + 1, :]
        home = jnp.sum(jnp.where(node_id == node, home_col, 0), axis=0, keepdims=True)
        other = lax.rem(home + jnp.maximum(second[j : j + 1, :], 1), 4)
        for k, pick in ((2 * j, home), (2 * j + 1, other)):
            weight = weights[k : k + 1, :].astype(F32)
            tail = tail + jnp.where(lane == node * 4 + pick, weight, 0.0)
    tail = tail.T.astype(BF)
    for out, is_left in ((keep, first), (send, jnp.logical_not(first))):
        out[:, :half] = jnp.where(is_left, tok[:, :half], tok[:, half:])
        out[:, half : half + TAIL] = tail
        out[:, half + TAIL :] = jnp.where(is_left, cot[:, :half], cot[:, half:])


def weight_kernel(core, gate, up, down, _, own, oth, down_own, down_oth, sems):
    half = down_own.shape[1]
    hid_width = gate.shape[1]
    copies = []
    for out, down_out, which in ((own, down_own, core[0]), (oth, down_oth, 1 - core[0])):
        place = pl.ds(pl.multiple_of(which * half, half), half)
        top = pl.ds(0, half)
        copies.append((gate.at[place, :], out.at[top, pl.ds(0, hid_width)]))
        copies.append((up.at[place, :], out.at[top, pl.ds(hid_width, hid_width)]))
        copies.append((down.at[:, place], down_out))
    copies = [
        pltpu.make_async_copy(src, dst, sems.at[i]) for i, (src, dst) in enumerate(copies)
    ]
    for copy in copies:
        copy.start()
    for out in (own, oth):
        out[half:, :] = jnp.zeros((out.shape[0] - half, out.shape[1]), BF)
    for copy in copies:
        copy.wait()


def stack_kernel(count, *refs):
    start = 0
    for ref in refs[:count]:
        refs[-1][pl.ds(start, ref.shape[0]), :] = ref[...]
        start += ref.shape[0]


def stack(parts, *done):
    shape = (sum(part.shape[0] for part in parts), parts[0].shape[1])
    return pl.pallas_call(
        functools.partial(stack_kernel, len(parts)),
        out_shape=jax.ShapeDtypeStruct(shape, BF),
        in_specs=vmem(len(parts) + len(done)),
        out_specs=vmem(1)[0],
        compiler_params=limit(6),
    )(*parts, *done)


def per_device(
    tokens, cotangent, node_routes, home_local, second_local, gate_weights, gate_w, up_w, down_w
):
    tok, width = tokens.shape
    half = width // 2
    top = gate_weights.shape[1]
    cap = 5
    experts = lax.axis_size("node") * 4
    node = lax.axis_index("node")
    local = lax.axis_index("local")
    x_pos, z_pos = node // 4, node % 4
    core = local % 2
    first = core == 0
    my_expert = 4 * node + local // 2
    core_arg = core.astype(jnp.int32).reshape(1)
    anywhere = pl.BlockSpec(memory_space=pl.ANY)

    raw_keep, raw_send = pl.pallas_call(
        start_kernel,
        out_shape=[jax.ShapeDtypeStruct((tok, width + TAIL), BF)] * 2,
        in_specs=[pl.BlockSpec(memory_space=pltpu.SMEM)] + [pl.BlockSpec()] * 6,
        out_specs=vmem(2),
    )(
        core_arg,
        tokens,
        cotangent,
        node_routes.T,
        home_local,
        second_local.T,
        gate_weights.T,
    )
    chip = jnp.concatenate([raw_keep, across(raw_send)], axis=0)
    rows = jnp.concatenate(
        [chip, along_x(chip, 1), along_x(chip, -1), along_x(chip, 2)], axis=0
    )

    weights = rows[:, half : half + experts]
    count = rows.shape[0]
    groups = count // tok
    slots = groups * cap
    nearby = 4 * x_pos + (z_pos + jnp.arange(4, dtype=jnp.int32)) % 4
    in_node = (jnp.arange(experts, dtype=jnp.int32)[:, None] // 4 == nearby[None, :]).astype(BF)
    member = nn((weights != 0).astype(BF), in_node) > 0
    row = jnp.arange(count, dtype=jnp.int32)
    before = (row[:, None] // tok == row[None, :] // tok) & (row[:, None] > row[None, :])
    rank = nn(before.astype(BF), member.astype(BF)).astype(jnp.int32)
    group = row // tok
    place = ((group // 2 * 2 + (group + core) % 2) * cap)[:, None] + rank
    place = jnp.where(member, place, -1)
    select = (
        (place.T[:, None, :] == jnp.arange(slots, dtype=jnp.int32)[None, :, None])
        .astype(BF)
        .reshape(4 * slots, count)
    )
    parts = jnp.split(nn(select, rows).astype(BF), 4, axis=0)
    side = 2 * slots

    hid_width = gate_w.shape[2]
    proj_own, proj_oth, down_own, down_oth = pl.pallas_call(
        weight_kernel,
        out_shape=[jax.ShapeDtypeStruct((half + TAIL, 2 * hid_width), BF)] * 2
        + [jax.ShapeDtypeStruct((hid_width, half), BF)] * 2,
        in_specs=[pl.BlockSpec(memory_space=pltpu.SMEM)]
        + [pl.BlockSpec(memory_space=pltpu.HBM)] * 3
        + [anywhere],
        out_specs=vmem(4),
        scratch_shapes=[pltpu.SemaphoreType.DMA((6,))],
        compiler_params=limit(14),
    )(core_arg, gate_w[0], up_w[0], down_w[0], raw_send)

    parts = exchange_z(parts, 1)
    first_below, first_above = along_y(parts[0], 1), along_y(parts[0], -1)
    rest = stack(parts[1:], first_below, first_above)
    mine = jnp.concatenate([parts[0], rest], axis=0)
    below = jnp.concatenate([first_below, along_y(rest, 1)], axis=0)
    above = jnp.concatenate([first_above, along_y(rest, -1)], axis=0)
    far_parts = along_y(below[:side], 1), along_y(above[side:], -1)
    near = [mine, below, above]
    tail_lane = jnp.arange(TAIL, dtype=jnp.int32)[None, :]

    def row_gradients(own, oth):
        x_own, d_own = own[:, : half + TAIL], own[:, half + TAIL :]
        x_oth, d_oth = oth[:, : half + TAIL], oth[:, half + TAIL :]
        weight = jnp.sum(
            jnp.where(tail_lane == my_expert, x_own[:, half:].astype(F32), 0.0),
            axis=1,
            keepdims=True,
        )
        pre = nn(x_own, proj_own) + nn(x_oth, proj_oth)
        pre_gate, pre_up = pre[:, :hid_width], pre[:, hid_width:]
        activated, slope = silu_parts(pre_gate)
        hidden = (activated * pre_up).astype(BF)
        scaled = (weight * hidden.astype(F32)).astype(BF)
        hidden, scaled, for_gate, for_up = lax.optimization_barrier(
            (hidden, scaled, weight * (pre_up * slope), weight * activated)
        )
        hidden_grad = nt(d_own, down_own) + nt(d_oth, down_oth)
        grads = jnp.concatenate(
            [(hidden_grad * for_gate).astype(BF), (hidden_grad * for_up).astype(BF)], axis=1
        )
        got = across(nt(grads, proj_oth[:half]).astype(BF))
        keep = nt(grads, proj_own[:half])
        router = jnp.sum(hidden_grad * hidden.astype(F32), axis=1)
        router = jnp.where(weight[:, 0] != 0, router, 0.0)
        router = (router + across(router))[:, None]
        high = router.astype(BF).astype(F32)
        tail = jnp.where(tail_lane == my_expert, high, 0.0)
        tail = jnp.where(tail_lane == my_expert + TAIL // 2, router - high, tail).astype(BF)
        full = jnp.concatenate([(keep + got.astype(F32)).astype(BF), tail], axis=1)
        return (own, oth, grads, scaled), full

    near_state, near_full = row_gradients(
        jnp.concatenate(near, axis=0), jnp.concatenate([across(p) for p in near], axis=0)
    )
    far = stack(far_parts, near_state[2])
    far_state, far_full = row_gradients(far, across(far))

    near_full, far_full = lax.optimization_barrier((near_full, far_full))
    own_top, own_bottom, below_top, below_bottom, above_top, above_bottom = jnp.split(
        near_full, 6, axis=0
    )
    from_above = along_y(jnp.concatenate([far_full[:side], below_bottom], axis=0), -1)
    from_below = along_y(jnp.concatenate([far_full[side:], above_top], axis=0), 1)
    early_top, early_bottom = from_below[side:], from_above[side:]
    late_top = along_y(below_top + from_above[:side], -1)
    late_bottom = along_y(above_bottom + from_below[:side], 1)

    def add(*parts):
        return sum(p.astype(F32) for p in parts).astype(BF)

    top_rows = add(own_top, early_top, late_top)
    bottom_rows = add(own_bottom, early_bottom, late_bottom)
    back = [top_rows[:slots], top_rows[slots:], bottom_rows[:slots], bottom_rows[slots:]]
    back = jnp.concatenate(exchange_z(back, -1), axis=0)
    parts = jnp.split(tn(select, back).astype(BF), 4, axis=0)
    parts = [parts[0], along_x(parts[1], -1), along_x(parts[2], 1), along_x(parts[3], 2)]
    chip = sum(p.astype(F32) for p in parts)
    theirs = across(chip[tok:, :half].astype(BF))
    mine = chip[:tok]
    mine_cols = mine[:, :half].astype(BF)
    d_tokens = jnp.concatenate(
        [jnp.where(first, mine_cols, theirs), jnp.where(first, theirs, mine_cols)], axis=1
    )
    by_expert = mine[:, half : half + TAIL // 2] + mine[:, half + TAIL // 2 :]
    by_expert = jnp.concatenate([by_expert, jnp.zeros_like(by_expert)], axis=1)
    lane16 = jnp.arange(home_local.shape[1], dtype=jnp.int32)
    node_match = node_routes[:, :, None] == lane16[None, None, :]
    home = jnp.sum(jnp.where(node_match, home_local[0][None, None, :], 0), axis=2)
    other = (home + jnp.maximum(second_local, 1)) % 4
    ids = jnp.repeat(node_routes, 2, axis=1) * 4 + jnp.stack([home, other], axis=2).reshape(tok, top)
    onehot = ids[:, :, None] == jnp.arange(TAIL, dtype=jnp.int32)[None, None, :]
    d_gates = jnp.sum(jnp.where(onehot, by_expert[:, None, :], 0.0), axis=2).astype(BF)

    own, oth, grads, scaled = [
        jnp.concatenate(both, axis=0)
        for both in zip(near_state, far_state)
    ]

    def whole(mine, theirs):
        return jnp.where(
            first,
            jnp.concatenate([mine, theirs], axis=1),
            jnp.concatenate([theirs, mine], axis=1),
        )

    x_all = whole(own[:, :half], oth[:, :half])
    d_all = whole(own[:, half + TAIL :], oth[:, half + TAIL :])
    return (
        d_tokens,
        d_gates,
        tn(x_all, grads[:, :hid_width]).astype(BF)[None],
        tn(x_all, grads[:, hid_width:]).astype(BF)[None],
        tn(scaled, d_all).astype(BF)[None],
    )


def solution(mesh):
    rows = P(("node", "local"), None)
    blocks = P(("node", "local"), None, None)
    return jax.shard_map(
        per_device,
        mesh=mesh,
        in_specs=(rows,) * 6 + (blocks,) * 3,
        out_specs=(rows, rows, blocks, blocks, blocks),
        check_vma=False,
    )
```
